128 devices in a mesh: gx: 8 (over z, core), gy: 16 (over y, x).
Axes of the slice: x: 4, y: 4, z: 4, core: 2. Of those that a mesh axis runs over, the one named last changes fastest.
Arguments:
- features: bfloat16 [512, 512, 256], P(('gx', 'gy')), may hold values from -6 to 6
- occupancy: int32 [512, 512], P(('gx', 'gy')), may hold values 0 or 1
- routes: int32 [512, 1], P(('gx', 'gy')), may hold values from 0 to 7; in each aligned block of 4 rows (0 to 3, 4 to 7, ...) no two rows name the same one
- neighbours: int32 [512, 6], P(('gx', 'gy')), may hold values from 0 to 8, as said below
- weight: bfloat16 [27, 256, 256], replicated, may hold values from -0.078125 to 0.078125
- cotangent: bfloat16 [1024, 512, 256], P(('gx', 'gy')), may hold values from -6 to 6
Outputs:
- owned_out: bfloat16 [1024, 512, 256], P(('gx', 'gy'))
- input_grad: bfloat16 [512, 512, 256], P(('gx', 'gy'))
- weight_grad: float32 [27, 256, 256], replicated
The draws below stay inside these ranges and needn't reach their ends.
Inputs may be any that keep to these rules, and one draw needn't show every extreme that they name: `routes`: at most 1 bricks of one device have the same owner, and some device gives exactly 1 to some owner. `neighbours`: values of the -z and +z columns are under 4 or exactly 8.
All inputs are finite; a program needn't handle non-finite values. No bound on the sum of `occupancy` on one device may be relied on, other than what follows from the above.
Results may differ from the reference program's by a relative error of at most 0.0029.
Values may be sent and summed in bfloat16 or wider, within the bound.
No kernel may reach another device: no remote copies, remote signals or barrier semaphores. Data moves between devices by JAX's collectives and lax.ppermute only.
A program may use at most 192 MiB of HBM per device.

```python
import math
import jax
import jax.numpy as jnp
import numpy as np
from jax import lax

C = 256
EDGE = 8
TAPS = 27
S = 4
MOST = 1
V = 512
FACE = 64
OSL = 8
BRICKS = 512
OWNED = 1024
N_GX = 8
N_GY = 16
DEVICES = 128


def draw_neighbours(key, part):
    key = jax.random.fold_in(key, 11)
    plane_key, depth_key = jax.random.split(key)
    planar = jax.random.randint(plane_key, (BRICKS, 4), 0, 2 * S + 1)
    vertical = jax.random.randint(depth_key, (BRICKS, 2), 0, S + 1)
    vertical = jnp.where(vertical == S, 2 * S, vertical)
    return jnp.concatenate([planar, vertical], axis=1).astype(jnp.int32)


def plant(drawn, key, low, largest):
    index_at = [jax.random.randint(jax.random.fold_in(key, axis), (), 0, length) for axis, length in enumerate(drawn.shape)]
    widest = drawn.shape.index(max(drawn.shape))
    next_to = index_at[:widest] + [(index_at[widest] + 1) % drawn.shape[widest]] + index_at[widest + 1:]
    return drawn.at[tuple(index_at)].set(low).at[tuple(next_to)].set(largest)


def levels(key, extent, shards, low, largest):
    loudness, own = 1.0, jax.random.fold_in(key, 6)
    for position, blocks in shards:
        draws = jnp.exp(jax.random.uniform(jax.random.fold_in(own, position), (blocks,), jnp.float32, low / len(shards), largest / len(shards)))
        loudness = loudness * jnp.repeat(draws, extent[position] // blocks).reshape([-1 if axis == position else 1 for axis in range(len(extent))])
    return loudness


def assign_block(stream_key, own, number, rows, amount, top, limit, skew):
    ranking = jax.random.permutation(stream_key, amount)
    heavy_load, usual = load_shares(amount, rows * top, limit, skew, True), load_shares(amount, rows * top, limit, skew, False)
    places = jnp.arange(amount)

    def named(sizes, offset_by):
        used = int((sizes > 0).sum())
        fixed = max(1, used // 4)
        moved = fixed + (places - fixed + offset_by * (used - fixed)) % max(1, amount - fixed)
        return jnp.zeros((amount,), jnp.int32).at[ranking[jnp.where(places < fixed, places, moved)]].set(jnp.asarray(sizes, jnp.int32))

    sizes = jnp.where(number % 4 == 0, named(heavy_load, number // 4), named(usual, number - number // 4 - 1))
    mixed = jax.random.permutation(jax.random.fold_in(own, 3), amount)
    source_of, receiver = mixed[0:amount // 2 * 2:2], mixed[1:amount // 2 * 2:2]
    room = jnp.minimum(sizes[source_of] - 1, limit - sizes[receiver]) // 2
    room = jnp.where((source_of == ranking[0]) | (receiver == ranking[0]) | (sizes[receiver] == 0), 0, jnp.maximum(room, 0))
    moved = jax.random.randint(jax.random.fold_in(own, 4), (amount // 2,), 0, 1 << 20) % (room + 1)
    sizes = sizes.at[source_of].add(-moved).at[receiver].add(moved)
    labels = jnp.searchsorted(jnp.cumsum(sizes), jnp.arange(rows * top), side="right").astype(jnp.int32)
    table = labels.reshape(top, rows).T
    table = table[jax.random.permutation(jax.random.fold_in(own, 1), rows)]
    offset_by = jax.random.randint(jax.random.fold_in(own, 2), (rows, 1), 0, top)
    return jnp.take_along_axis(table, (jnp.arange(top)[None, :] + offset_by) % top, axis=1)


def load_shares(number_of, total, limit, slope, full):
    portions = [(1 << 20) // math.isqrt(rank ** slope) + 1 for rank in range(1, number_of + 1)]
    largest = limit if full else min(limit, max(-(-total // number_of), total * portions[0] // sum(portions)))
    least = 1 if total - largest >= number_of - 1 else 0
    given, rest = [largest] + [least] * (number_of - 1), total - largest - least * (number_of - 1)
    while rest > 0:
        movable = [i for i in range(1, number_of) if given[i] < largest] or [i for i in range(1, number_of) if given[i] < limit]
        whole, remaining = sum([portions[i] for i in movable]), rest
        for i in movable:
            more = min(limit - given[i], max(1, remaining * portions[i] // whole), rest)
            given[i] = given[i] + more
            rest = rest - more
    return np.array(given)


def centred(stream_key, dims, scale, reach, shards=(), kind=jnp.bfloat16):
    gain = levels(stream_key, dims, shards, -0.22, 0.18) if shards else 1.0
    values = jax.random.normal(stream_key, dims, jnp.float32) * scale * gain
    return jnp.minimum(jnp.maximum(values, -reach), reach).astype(kind)


def setup_inputs(seed: int = 0) -> dict:
    keys = jax.random.split(jax.random.key(seed), 7)
    features = centred(keys[0], (BRICKS, V, C), 1.0, 6.0, ((0, 128),))
    occupancy = plant((jax.random.randint(keys[1], (BRICKS, V), 0, 5) < 3).astype(jnp.int32), jax.random.fold_in(keys[1], 1), 0, 1)
    routes_keys = jax.random.split(jax.random.fold_in(keys[2], 1), BRICKS // S)
    routes_turns = jax.random.permutation(jax.random.fold_in(keys[2], 3), BRICKS // S)
    routes = jax.vmap(lambda own, number: assign_block(jax.random.fold_in(keys[2], 2), own, number, S, N_GX, 1, MOST, 2))(routes_keys, routes_turns).reshape((BRICKS, 1))
    neighbours = draw_neighbours(jax.random.fold_in(keys[6], 71), 0)
    weight = centred(keys[4], (TAPS, C, C), (TAPS * C) ** -0.5, 0.078125)
    cotangent = centred(keys[5], (OWNED, V, C), 1.0, 6.0, ((0, 128),))
    return dict(features=features, occupancy=occupancy, routes=routes, neighbours=neighbours, weight=weight, cotangent=cotangent)


norm_eps = 1e-06
face_steps = ((-1, 0), (1, 0), (0, -1), (0, 1))

def hidden_of(values, occupancy):
    scale = lax.rsqrt(lax.optimization_barrier(jnp.mean(values * values, axis=-1, keepdims=True)) + norm_eps)
    return occupancy[..., None].astype(jnp.float32) * jax.nn.silu(values * scale)

def layer_of(cube, layer_id):
    edge_cells = cube.shape[1]
    side_pos = 0 if layer_id % 2 == 0 else edge_cells - 1
    if layer_id < 2:
        return cube[:, side_pos]
    if layer_id < 4:
        return cube[:, :, side_pos]
    return cube[:, :, :, side_pos]

def add_layer(cube, layer_id, addend):
    edge_cells = cube.shape[1]
    side_pos = 0 if layer_id % 2 == 0 else edge_cells - 1
    if layer_id < 2:
        return cube.at[:, side_pos].add(addend)
    if layer_id < 4:
        return cube.at[:, :, side_pos].add(addend)
    return cube.at[:, :, :, side_pos].add(addend)

def padded_of(cube, faces):
    edge_cells = cube.shape[1]
    inside = slice(1, edge_cells + 1)
    padded = jnp.pad(cube, ((0, 0), (1, 1), (1, 1), (1, 1), (0, 0)))
    padded = padded.at[:, 0, inside, inside].set(faces[0])
    padded = padded.at[:, edge_cells + 1, inside, inside].set(faces[1])
    padded = padded.at[:, inside, 0, inside].set(faces[2])
    padded = padded.at[:, inside, edge_cells + 1, inside].set(faces[3])
    padded = padded.at[:, inside, inside, 0].set(faces[4])
    padded = padded.at[:, inside, inside, edge_cells + 1].set(faces[5])
    return padded

def face_taps(face_id):
    axis_id = face_id // 2
    fixed_tap = 0 if face_id % 2 == 0 else 2
    listing = []
    for tap_a in range(3):
        for tap_b in range(3):
            coords = [tap_a, tap_b]
            coords.insert(axis_id, fixed_tap)
            listing.append((coords[0] * 9 + coords[1] * 3 + coords[2], tap_a, tap_b))
    return listing

def face_slab(grad_grid, face_id, tap_a, tap_b, edge_cells):
    axis_id = face_id // 2
    fixed_pos = 2 if face_id % 2 == 0 else edge_cells + 1
    first_cut = slice(3 - tap_a, 3 - tap_a + edge_cells)
    second_cut = slice(3 - tap_b, 3 - tap_b + edge_cells)
    if axis_id == 0:
        return grad_grid[:, fixed_pos, first_cut, second_cut]
    if axis_id == 1:
        return grad_grid[:, first_cut, fixed_pos, second_cut]
    return grad_grid[:, first_cut, second_cut, fixed_pos]

def reference(features, occupancy, routes, neighbours, weight, cotangent):
    count = features.shape[0]
    width = features.shape[2]
    values = features.astype(jnp.float32)
    hidden = hidden_of(values, occupancy).astype(jnp.bfloat16)
    cube = hidden.reshape(count, EDGE, EDGE, EDGE, width)
    device = jnp.arange(count, dtype=jnp.int32) // S
    row_id = device // N_GY
    col_id = device % N_GY
    targets = []
    for face_id in range(6):
        entry = neighbours[:, face_id]
        target = jnp.where(entry < S, device * S + entry, count)
        if face_id < 4:
            step_row, step_col = face_steps[face_id]
            near_row = row_id + step_row
            near_col = col_id + step_col
            inside = (near_row >= 0) & (near_row < N_GX) & (near_col >= 0) & (near_col < N_GY)
            remote = (entry >= S) & (entry < 2 * S) & inside
            target = jnp.where(remote, (near_row * N_GY + near_col) * S + entry - S, target)
        targets.append(target.astype(jnp.int32))
    blank = jnp.zeros((1, EDGE, EDGE, width), jnp.bfloat16)
    faces = []
    for face_id in range(6):
        table = jnp.concatenate([layer_of(cube, face_id ^ 1), blank], axis=0)
        faces.append(table[targets[face_id]])
    padded = padded_of(cube, faces)
    route = routes[:, 0]
    grouped = route.reshape(DEVICES, S)
    same = grouped[:, :, None] == grouped[:, None, :]
    earlier = jnp.arange(S)[None, :] < jnp.arange(S)[:, None]
    rank = lax.optimization_barrier(jnp.sum(same & earlier[None], axis=2)).astype(jnp.int32).reshape(count)
    owner_row = ((route * N_GY + col_id) * OSL + row_id * MOST + rank).astype(jnp.int32)
    grad_in = cotangent[owner_row]
    dmixed = grad_in * occupancy[..., None].astype(jnp.bfloat16)
    flat_rows = count * V
    dmixed_flat = dmixed.reshape(flat_rows, width)
    grad_grid = jnp.pad(dmixed.reshape(count, EDGE, EDGE, EDGE, width), ((0, 0), (2, 2), (2, 2), (2, 2), (0, 0)))
    mixed = jnp.zeros((flat_rows, width), jnp.float32)
    inner_grad = jnp.zeros((flat_rows, width), jnp.float32)
    kernel_grads = []
    for tap_x in range(3):
        for tap_y in range(3):
            for tap_z in range(3):
                tap_id = tap_x * 9 + tap_y * 3 + tap_z
                window = padded[:, tap_x:tap_x + EDGE, tap_y:tap_y + EDGE, tap_z:tap_z + EDGE].reshape(flat_rows, width)
                mixed = mixed + jnp.dot(window, weight[tap_id], preferred_element_type=jnp.float32)
                kernel_grads.append(jnp.dot(window.T, dmixed_flat, preferred_element_type=jnp.float32))
                shifted = grad_grid[:, 3 - tap_x:3 - tap_x + EDGE, 3 - tap_y:3 - tap_y + EDGE, 3 - tap_z:3 - tap_z + EDGE].reshape(flat_rows, width)
                inner_grad = inner_grad + jnp.dot(shifted, weight[tap_id].T, preferred_element_type=jnp.float32)
    face_grads = []
    for face_id in range(6):
        total_face = jnp.zeros((count * FACE, width), jnp.float32)
        for tap_id, tap_a, tap_b in face_taps(face_id):
            slab = face_slab(grad_grid, face_id, tap_a, tap_b, EDGE).reshape(count * FACE, width)
            total_face = total_face + jnp.dot(slab, weight[tap_id].T, preferred_element_type=jnp.float32)
        rounded = lax.optimization_barrier(total_face.astype(jnp.bfloat16))
        face_grads.append(rounded.reshape(count, EDGE, EDGE, width))
    output = (values + occupancy[..., None].astype(jnp.float32) * mixed.reshape(count, V, width)).astype(jnp.bfloat16)
    owned_out = jnp.zeros((DEVICES * OSL, V, width), jnp.bfloat16).at[owner_row].set(output)
    inner_round = lax.optimization_barrier(inner_grad.astype(jnp.bfloat16))
    dcube = inner_round.astype(jnp.float32).reshape(count, EDGE, EDGE, EDGE, width)
    for face_id in range(6):
        landed = jnp.zeros((count + 1, EDGE, EDGE, width), jnp.float32)
        landed = landed.at[targets[face_id]].add(face_grads[face_id].astype(jnp.float32))
        dcube = add_layer(dcube, face_id ^ 1, landed[:count])
    dhidden = dcube.reshape(count, V, width)
    _, pullback = jax.vjp(lambda inputs: hidden_of(inputs, occupancy), values)
    input_grad = (grad_in.astype(jnp.float32) + pullback(dhidden)[0]).astype(jnp.bfloat16)
    weight_grad = jnp.stack(kernel_grads) * float(count * V) ** (-0.5)
    return (owned_out, input_grad, weight_grad)
```

```python
import jax
import jax.numpy as jnp
from jax import lax
from jax.experimental import pallas as pl
from jax.experimental.pallas import tpu as pltpu
from jax.sharding import PartitionSpec as P

EDGE = 8
TAPS = 27
V = 512
FACE = 64
PLANE = 80
MIB = 1 << 20

norm_eps = 1e-06


def from_behind(block, axis, distance):
    count = lax.axis_size(axis)
    return lax.ppermute(block, axis, [(i, (i + distance) % count) for i in range(count)])


def inner_neighbours(neighbours, listed):
    p, q = lax.axis_index("gx"), lax.axis_index("gy")
    inside = jnp.stack(
        [p > 0, p < lax.axis_size("gx") - 1, q > 0, q < lax.axis_size("gy") - 1, True, True]
    )
    return jnp.where(inside[None, :] | (neighbours < listed), neighbours, 2 * listed)


def hop(blocks, sign):
    count = lax.axis_size("gx")
    ways = [
        (p, (p // 2 + (sign if p % 2 == 0 else -sign)) * 2 % count + p % 2)
        for p in range(count)
    ]
    return lax.ppermute(blocks, "gx", ways)


def to_other_core(block):
    return lax.ppermute(block, "gx", [(p, p ^ 1) for p in range(lax.axis_size("gx"))])


def params(limit):
    return pltpu.CompilerParams(vmem_limit_bytes=limit * MIB)


def whole(shape):
    zeros = (0,) * len(shape)
    return pl.BlockSpec(shape, lambda *_: zeros)


def by_brick(shape):
    zeros = (0,) * len(shape)
    return pl.BlockSpec((1,) + shape, lambda s, *_: (s,) + zeros)


def smem():
    return pl.BlockSpec(memory_space=pltpu.SMEM)


def anywhere():
    return pl.BlockSpec(memory_space=pl.ANY)


def mask_of(occ_row, width):
    spread = jnp.broadcast_to(occ_row.astype(jnp.float32), (128, V))
    column = jnp.transpose(spread)
    return jnp.concatenate([column] * (width // 128), axis=1)


def norm_scale(values):
    return lax.rsqrt(jnp.mean(values * values, axis=-1, keepdims=True) + norm_eps)


def sigmoid(u):
    return 1.0 / (1.0 + jnp.exp(-u))


def hidden_kernel(feat_ref, occ_ref, hid_ref, x0_ref, x1_ref, y0_ref, y1_ref):
    width = feat_ref.shape[2]
    values = feat_ref[0].astype(jnp.float32)
    u = values * norm_scale(values)
    hidden = mask_of(occ_ref[0], width) * (u * sigmoid(u))
    hid_ref[0] = hidden.astype(jnp.bfloat16)
    cube = hidden.reshape(EDGE, EDGE, EDGE, width)
    x0_ref[0] = cube[0].reshape(FACE, width).astype(jnp.bfloat16)
    x1_ref[0] = cube[EDGE - 1].reshape(FACE, width).astype(jnp.bfloat16)
    y0_ref[0] = cube[:, 0].reshape(FACE, width).astype(jnp.bfloat16)
    y1_ref[0] = cube[:, EDGE - 1].reshape(FACE, width).astype(jnp.bfloat16)


def hidden_call(features, occ_rows):
    listed, _, width = features.shape
    layer = jax.ShapeDtypeStruct((listed, FACE, width), jnp.bfloat16)
    return pl.pallas_call(
        hidden_kernel,
        grid=(listed,),
        in_specs=[by_brick((V, width)), by_brick((1, V))],
        out_specs=[by_brick((V, width))] + [by_brick((FACE, width))] * 4,
        out_shape=[jax.ShapeDtypeStruct((listed, V, width), jnp.bfloat16)] + [layer] * 4,
        compiler_params=params(16),
        name="hidden",
    )(features, occ_rows)


def hold_kernel(*refs):
    pass


def hold_call(blocks, after):
    return pl.pallas_call(
        hold_kernel,
        in_specs=[anywhere()] * (len(blocks) + len(after)),
        out_specs=[anywhere()] * len(blocks),
        out_shape=[jax.ShapeDtypeStruct(block.shape, block.dtype) for block in blocks],
        input_output_aliases={i: i for i in range(len(blocks))},
        compiler_params=params(16),
        name="hold",
    )(*blocks, *after)


def collect_kernel(place_ref, own_ref, near_ref, far_ref, back_ref, mate_ref, out_ref):
    for step, came_ref in enumerate((own_ref, near_ref, far_ref, back_ref)):
        out_ref[place_ref[2 * step]] = came_ref[0]
        out_ref[place_ref[2 * step + 1]] = mate_ref[step]


def collect_call(place, own, near, far, back, mate):
    shape = (2 * mate.shape[0],) + mate.shape[1:]
    return pl.pallas_call(
        collect_kernel,
        grid=(1,),
        in_specs=[smem()] + [whole(own.shape)] * 4 + [whole(mate.shape)],
        out_specs=whole(shape),
        out_shape=jax.ShapeDtypeStruct(shape, mate.dtype),
        compiler_params=params(20),
        name="collect",
    )(place, own, near, far, back, mate)


def roll_c(block, shift):
    flat = block.reshape((-1,) + block.shape[-2:])
    return pltpu.roll(flat, shift % EDGE, 1).reshape(block.shape)


def c_index(shape):
    return lax.broadcasted_iota(jnp.int32, shape, len(shape) - 2)


def extended_brick(s, near_ref, hid_ref, own, far, store):
    listed, _, width = hid_ref.shape

    def flag(condition):
        return jnp.where(condition, 1.0, 0.0).astype(jnp.float32)

    def face(f):
        n = near_ref[s, f]
        here = own[f ^ 1][jnp.minimum(n, listed - 1)].astype(jnp.float32)
        there = far[f][jnp.clip(n - listed, 0, listed - 1)].astype(jnp.float32)
        value = here * flag(n < listed) + there * flag((n >= listed) & (n < 2 * listed))
        return value.reshape(EDGE, EDGE, width)

    def column(f):
        n = near_ref[s, f]
        brick = hid_ref[jnp.minimum(n, listed - 1)].astype(jnp.float32) * flag(n < listed)
        return brick.reshape(EDGE, EDGE, EDGE, width)

    def extended(core, sides):
        x0, x1, y0, y1 = sides
        blank = jnp.zeros((1, EDGE, width), jnp.float32)
        middle = jnp.concatenate([y0[:, None], core, y1[:, None]], axis=1)
        first = jnp.concatenate([blank, x0, blank], axis=0)[None]
        last = jnp.concatenate([blank, x1, blank], axis=0)[None]
        return jnp.concatenate([first, middle, last], axis=0)

    def put(k, block):
        everything = block.reshape(EDGE + 2, PLANE, width).astype(jnp.bfloat16)
        inner = block[:, 1 : EDGE + 1].reshape(EDGE + 2, FACE, width).astype(jnp.bfloat16)
        store(k, everything, inner)

    core = hid_ref[s].astype(jnp.float32).reshape(EDGE, EDGE, EDGE, width)
    sides = [face(f) for f in range(4)]
    at = c_index(core.shape)
    at_side = c_index(sides[0].shape)
    for k, edge, f in ((0, EDGE - 1, 4), (2, 0, 5)):
        shown = extended(
            jnp.where(at == edge, column(f), core),
            [jnp.where(at_side == edge, 0.0, side) for side in sides],
        )
        put(k, roll_c(shown, 1 - k))
    put(1, extended(core, sides))


def window(even_ref, odd_ref, s, i, j, k):
    if j == 1:
        part = odd_ref[s, k, pl.ds(i, EDGE)]
    else:
        part = even_ref[s, k, pl.ds(i, EDGE), j * EDGE : j * EDGE + FACE]
    return part.reshape(V, part.shape[-1])


def forward_kernel(
    near_ref, place_ref, hid_ref, l0, l1, l2, l3, r0, r1, r2, r3, feat_ref, occ_ref, w_ref,
    *refs,
):
    outs, even_ref, odd_ref = refs[:-2], refs[-2], refs[-1]
    s = pl.program_id(0)
    width = feat_ref.shape[2]

    @pl.when(s == 0)
    def _():
        for out_ref in outs:
            out_ref[...] = jnp.zeros_like(out_ref)

    def store(k, everything, inner):
        even_ref[0, k] = everything
        odd_ref[0, k] = inner

    extended_brick(s, near_ref, hid_ref, (l0, l1, l2, l3), (r0, r1, r2, r3), store)
    total = jnp.zeros((V, width), jnp.float32)
    for i in range(3):
        for j in range(3):
            rows = jnp.concatenate(
                [window(even_ref, odd_ref, 0, i, j, k) for k in range(3)], axis=1
            )
            total = total + jnp.dot(rows, w_ref[3 * i + j], preferred_element_type=jnp.float32)
    result = feat_ref[0].astype(jnp.float32) + mask_of(occ_ref[0], width) * total
    result = result.astype(jnp.bfloat16)
    for step, out_ref in enumerate(outs):

        @pl.when(place_ref[s] // 2 == step)
        def _():
            out_ref[place_ref[s] % 2] = result


def extended_scratch(bricks, width):
    return [
        pltpu.VMEM((bricks, 3, EDGE + 2, PLANE, width), jnp.bfloat16),
        pltpu.VMEM((bricks, 3, EDGE + 2, FACE, width), jnp.bfloat16),
    ]


def forward_call(neighbours, place, hidden, layers, remote, features, occ_rows, weight9, slots):
    listed, _, width = features.shape
    layer = whole((listed, FACE, width))
    return pl.pallas_call(
        forward_kernel,
        grid=(listed,),
        in_specs=[smem(), smem(), whole((listed, V, width))]
        + [layer] * 8
        + [by_brick((V, width)), by_brick((1, V)), whole(weight9.shape)],
        out_specs=[whole((2, V, width))] * (slots // 2),
        out_shape=[jax.ShapeDtypeStruct((2, V, width), jnp.bfloat16)] * (slots // 2),
        scratch_shapes=extended_scratch(1, width),
        compiler_params=params(56),
        cost_estimate=pl.CostEstimate(
            flops=2 * listed * V * TAPS * width * width,
            bytes_accessed=10 * MIB,
            transcendentals=0,
        ),
        name="forward",
    )(neighbours, place, hidden, *layers, *remote, features, occ_rows, weight9)


def weight_kernel(
    near_ref, place_ref, core_ref, hid_ref, l0, l1, l2, l3, r0, r1, r2, r3, occ_ref, after_ref,
    *refs, scale,
):
    came, refs = refs[:-7], refs[-7:]
    mine_ref, theirs_ref, grad_ref, even_ref, odd_ref, turned_ref, sem = refs
    part = V // len(came)
    i = pl.program_id(0)
    listed, _, width = hid_ref.shape
    half = width // 2

    def copy(t, s):
        return pltpu.make_async_copy(
            came[t].at[place_ref[s, 0]],
            grad_ref.at[s, pl.ds(t * part, part)],
            sem.at[t * listed + s],
        )

    @pl.when(i == 0)
    def _():
        for s in range(listed):
            for t in range(len(came)):
                copy(t, s).start()

        @pl.loop(0, listed)
        def _(s):
            def store(k, everything, inner):
                even_ref[s, k] = everything
                odd_ref[s, k] = inner

            extended_brick(s, near_ref, hid_ref, (l0, l1, l2, l3), (r0, r1, r2, r3), store)

        for s in range(listed):
            for t in range(len(came)):
                copy(t, s).wait()
            mixed = grad_ref[s].astype(jnp.float32) * mask_of(occ_ref[s], width)
            turned_ref[:, s * V : (s + 1) * V] = jnp.transpose(mixed).astype(jnp.bfloat16)

    @pl.when(i < 3)
    def _():
        first = core_ref[0] == 0
        for j in range(3):
            for k in range(3):
                rows = jnp.concatenate(
                    [window(even_ref, odd_ref, s, i, j, k) for s in range(listed)], axis=0
                )
                product = jnp.dot(turned_ref[...], rows, preferred_element_type=jnp.float32)
                product = jnp.transpose(product) * scale
                low, high = product[:, :half], product[:, half:]
                mine_ref[3 * j + k] = jnp.where(first, low, high)
                theirs_ref[3 * j + k] = jnp.where(first, high, low).astype(theirs_ref.dtype)

    @pl.when(i == 3)
    def _():
        mine_ref[...] = jnp.zeros_like(mine_ref)
        theirs_ref[...] = jnp.zeros_like(theirs_ref)


def weight_call(
    neighbours, place, core, hidden, layers, remote, came, occ_rows, scale, kind, after
):
    listed, _, width = hidden.shape
    shape = (TAPS + 1, width, width // 2)
    block = pl.BlockSpec((9, width, width // 2), lambda i: (i, 0, 0))
    return pl.pallas_call(
        lambda *refs: weight_kernel(*refs, scale=scale),
        grid=(4,),
        in_specs=[smem(), smem(), smem(), whole(hidden.shape)]
        + [whole((listed, FACE, width))] * 8
        + [whole(occ_rows.shape), anywhere()]
        + [anywhere()] * len(came),
        out_specs=[block, block, whole(hidden.shape)],
        out_shape=[
            jax.ShapeDtypeStruct(shape, jnp.float32),
            jax.ShapeDtypeStruct(shape, kind),
            jax.ShapeDtypeStruct(hidden.shape, jnp.bfloat16),
        ],
        scratch_shapes=extended_scratch(listed, width)
        + [pltpu.VMEM((width, listed * V), jnp.bfloat16), pltpu.SemaphoreType.DMA((len(came) * listed,))],
        compiler_params=params(32),
        cost_estimate=pl.CostEstimate(
            flops=2 * listed * V * TAPS * width * width,
            bytes_accessed=10 * MIB,
            transcendentals=0,
        ),
        name="weight_gradient",
    )(neighbours, place, core, hidden, *layers, *remote, occ_rows, after, *came)


def chip_kernel(mine_ref, theirs_ref, *refs):
    out_ref = refs[-1]
    added = mine_ref[...] + theirs_ref[...].astype(jnp.float32)
    out_ref[...] = added.astype(jnp.bfloat16)


def chip_call(mine, theirs, after):
    taps, width, half = mine.shape
    block = pl.BlockSpec((7, width, half), lambda t: (t, 0, 0))
    return pl.pallas_call(
        chip_kernel,
        grid=(taps // 7,),
        in_specs=[block, block] + [anywhere()] * len(after),
        out_specs=block,
        out_shape=jax.ShapeDtypeStruct(mine.shape, jnp.bfloat16),
        compiler_params=params(12),
        name="chip_sum",
    )(mine, theirs, *after)


def total_kernel(parts_ref, *refs):
    out_ref = refs[-1]
    total = jnp.sum(parts_ref[...].astype(jnp.float32), axis=0)
    for z in range(out_ref.shape[0]):
        out_ref[z] = total.astype(jnp.bfloat16)


def total_call(parts, copies, after):
    _, rows, half = parts.shape
    return pl.pallas_call(
        total_kernel,
        grid=(1,),
        in_specs=[whole(parts.shape)] + [anywhere()] * len(after),
        out_specs=whole((copies, rows, half)),
        out_shape=jax.ShapeDtypeStruct((copies, rows, half), jnp.bfloat16),
        compiler_params=params(20),
        name="total",
    )(parts, *after)


def join_kernel(core_ref, own_ref, other_ref, after_ref, out_ref):
    half = own_ref.shape[2]
    first = core_ref[0] == 0

    def put(low_ref, high_ref):
        out_ref[:, :, :half] = low_ref[...].astype(jnp.float32)
        out_ref[:, :, half:] = high_ref[...].astype(jnp.float32)

    @pl.when(first)
    def _():
        put(own_ref, other_ref)

    @pl.when(jnp.logical_not(first))
    def _():
        put(other_ref, own_ref)


def join_call(core, own, other, after):
    _, width, half = own.shape
    block = pl.BlockSpec((9, width, half), lambda t: (t, 0, 0))
    return pl.pallas_call(
        join_kernel,
        grid=(TAPS // 9,),
        in_specs=[smem(), block, block, anywhere()],
        out_specs=pl.BlockSpec((9, width, 2 * half), lambda t: (t, 0, 0)),
        out_shape=jax.ShapeDtypeStruct((TAPS, width, 2 * half), jnp.float32),
        compiler_params=params(16),
        name="join",
    )(core, own, other, after)


def data_kernel(
    near_ref, buf_ref, occ_ref, w_ref, after_ref,
    grad_ref, s0_ref, s1_ref, s2_ref, s3_ref,
    wide_ref, rows_ref, depth_ref, kept_ref,
):
    s = pl.program_id(0)
    listed = grad_ref.shape[0]
    width = buf_ref.shape[2]
    last = s == listed - 1

    mixed = buf_ref[0].astype(jnp.float32) * mask_of(occ_ref[0], width)
    cube = mixed.reshape(FACE, EDGE, width)
    at = c_index(cube.shape)

    def three(block, index):
        ahead = jnp.where(index == EDGE - 1, 0.0, roll_c(block, -1))
        behind = jnp.where(index == 0, 0.0, roll_c(block, 1))
        flat = (-1, width)
        return [entry.reshape(flat).astype(jnp.bfloat16) for entry in (ahead, block, behind)]

    def back(rows, taps):
        return sum(
            lax.dot_general(
                row, w_ref[tap], (((1,), (1,)), ((), ())), preferred_element_type=jnp.float32
            )
            for row, tap in zip(rows, taps)
        )

    rows = three(cube, at)
    wide_ref[...] = jnp.zeros_like(wide_ref)
    for i in range(3):
        for j in range(3):
            product = back(rows, [9 * i + 3 * j + k for k in range(3)])
            wide_ref[i : i + EDGE, j * EDGE : j * EDGE + FACE] += product.reshape(
                EDGE, FACE, width
            )

    def rounded(block):
        return block.astype(jnp.bfloat16).astype(jnp.float32)

    inside = slice(EDGE, EDGE + FACE)
    grad_ref[s] = rounded(wide_ref[1 : EDGE + 1, inside].reshape(V, width))
    kept_ref[s, 0] = rounded(wide_ref[0, inside])
    kept_ref[s, 1] = rounded(wide_ref[EDGE + 1, inside])
    kept_ref[s, 2] = rounded(wide_ref[1 : EDGE + 1, 0:EDGE].reshape(FACE, width))
    kept_ref[s, 3] = rounded(wide_ref[1 : EDGE + 1, PLANE - EDGE : PLANE].reshape(FACE, width))

    halves = range(width // 128)
    for half in halves:
        rows_ref[half] = mixed[:, half * 128 : (half + 1) * 128]
    for side, c in ((0, 0), (1, EDGE - 1)):
        layer = jnp.concatenate(
            [rows_ref[half, pl.ds(c, FACE, stride=EDGE)] for half in halves], axis=1
        )
        layer = layer.reshape(EDGE, EDGE, width)
        for j, entry in enumerate(three(layer, c_index(layer.shape))):
            depth_ref[side, j, pl.ds(s * FACE, FACE)] = entry

    @pl.when(last)
    def _():
        sends = (s0_ref, s1_ref, s2_ref, s3_ref)
        for side in range(2):
            total = jnp.zeros((listed, EDGE + 2, EDGE, width), jnp.float32)
            for i in range(3):
                product = back(
                    [depth_ref[side, j] for j in range(3)],
                    [9 * i + 3 * j + 2 * side for j in range(3)],
                ).reshape(listed, EDGE, EDGE, width)
                pieces = [product]
                if i > 0:
                    pieces.insert(0, jnp.zeros((listed, i, EDGE, width), jnp.float32))
                if i < 2:
                    pieces.append(jnp.zeros((listed, 2 - i, EDGE, width), jnp.float32))
                total = total + jnp.concatenate(pieces, axis=1)
            rows_ref[...] = jnp.zeros_like(rows_ref)
            for h in range(listed):
                n = near_ref[h, 4 + side]

                @pl.when(n < listed)
                def _():
                    piece = rounded(total[h, 1 : EDGE + 1].reshape(FACE, width))
                    c = (EDGE - 1) * (1 - side)
                    for half in halves:
                        rows_ref[half, pl.ds(c, FACE, stride=EDGE)] = piece[
                            :, half * 128 : (half + 1) * 128
                        ]
                    grad_ref[n] += jnp.concatenate([rows_ref[half] for half in halves], axis=1)

        for f in range(4):
            sums = [jnp.zeros((FACE, width), jnp.float32) for _ in range(listed)]
            for h in range(listed):
                n = near_ref[h, f]
                piece = kept_ref[h, f]
                sums = [
                    total + piece * jnp.where(n == listed + t, 1.0, 0.0).astype(jnp.float32)
                    for t, total in enumerate(sums)
                ]

                @pl.when(n < listed)
                def _():
                    add_face(grad_ref, n, f, piece)

            for t in range(listed):
                sends[f][t] = sums[t].astype(jnp.bfloat16)


def add_face(ref, n, f, piece):
    near_end = f % 2 == 1
    if f < 2:
        start = 0 if near_end else V - FACE
        ref[n, start : start + FACE] += piece
    else:
        for a in range(EDGE):
            start = a * FACE + (0 if near_end else FACE - EDGE)
            ref[n, start : start + EDGE] += piece[a * EDGE : (a + 1) * EDGE]


def data_call(neighbours, grad_in, occ_rows, weight, after):
    listed, _, width = grad_in.shape
    layer = jax.ShapeDtypeStruct((listed, FACE, width), jnp.bfloat16)
    return pl.pallas_call(
        data_kernel,
        grid=(listed,),
        in_specs=[
            smem(), by_brick((V, width)), by_brick((1, V)), whole(weight.shape), anywhere()
        ],
        out_specs=[whole((listed, V, width))] + [whole(layer.shape)] * 4,
        out_shape=[jax.ShapeDtypeStruct((listed, V, width), jnp.float32)] + [layer] * 4,
        scratch_shapes=[
            pltpu.VMEM((EDGE + 2, PLANE, width), jnp.float32),
            pltpu.VMEM((width // 128, V, 128), jnp.float32),
            pltpu.VMEM((2, 3, listed * FACE, width), jnp.bfloat16),
            pltpu.VMEM((listed, 4, FACE, width), jnp.float32),
        ],
        compiler_params=params(32),
        cost_estimate=pl.CostEstimate(
            flops=2 * listed * V * (TAPS + 3) * width * width,
            bytes_accessed=10 * MIB,
            transcendentals=0,
        ),
        name="data_gradient",
    )(neighbours, grad_in, occ_rows, weight, after)


def finish_kernel(
    grad_ref, r0, r1, r2, r3, feat_ref, occ_ref, buf_ref, after_ref, out_ref, work_ref
):
    width = feat_ref.shape[2]
    work_ref[...] = grad_ref[...]
    for f, far in enumerate((r0, r1, r2, r3)):
        add_face(work_ref, 0, f, far[0].astype(jnp.float32))
    values = feat_ref[0].astype(jnp.float32)
    r = norm_scale(values)
    u = values * r
    sig = sigmoid(u)
    d_u = mask_of(occ_ref[0], width) * work_ref[0] * (sig * (1.0 + u * (1.0 - sig)))
    pulled = r * (d_u - u * jnp.mean(u * d_u, axis=-1, keepdims=True))
    out_ref[0] = (buf_ref[0].astype(jnp.float32) + pulled).astype(jnp.bfloat16)


def finish_call(grad, remote, features, occ_rows, grad_in, after):
    listed, _, width = features.shape
    return pl.pallas_call(
        finish_kernel,
        grid=(listed,),
        in_specs=[by_brick((V, width))]
        + [by_brick((FACE, width))] * 4
        + [by_brick((V, width)), by_brick((1, V)), by_brick((V, width)), anywhere()],
        out_specs=by_brick((V, width)),
        out_shape=jax.ShapeDtypeStruct((listed, V, width), jnp.bfloat16),
        scratch_shapes=[pltpu.VMEM((1, V, width), jnp.float32)],
        compiler_params=params(16),
        name="input_gradient",
    )(grad, *remote, features, occ_rows, grad_in, after)


def body(features, occupancy, routes, neighbours, weight, cotangent):
    listed, _, width = features.shape
    slots = cotangent.shape[0]
    rows, columns = lax.axis_size("gx"), lax.axis_size("gy")
    depth = rows // 2
    p = lax.axis_index("gx").astype(jnp.int32)
    z, c = p // 2, p % 2
    core = c.reshape(1)
    occ_rows = occupancy.reshape(listed, 1, V)
    neighbours = inner_neighbours(neighbours, listed)
    steps = jnp.arange(slots, dtype=jnp.int32)
    def way_of(core_id):
        return 1 - 2 * core_id

    source_core = (c + steps) % 2
    from_place = (z - way_of(source_core) * (steps // 2)) % depth * 2 + source_core
    route = routes[:, 0]
    out_place = way_of(c) * (route // 2 - z) % depth * 2 + (route + c) % 2

    hidden, *layers = hidden_call(features, occ_rows)
    remote = [
        from_behind(layers[1], "gx", 1),
        from_behind(layers[0], "gx", -1),
        from_behind(layers[3], "gy", 1),
        from_behind(layers[2], "gy", -1),
    ]
    lower, upper = cotangent[:, : V // 2], cotangent[:, V // 2 :]
    upper = hold_call([upper], remote[:2])[0]
    came = [lax.all_to_all(part, "gx", 0, 0, tiled=True) for part in (lower, upper)]
    placed = forward_call(
        neighbours, out_place, hidden, layers, remote, features, occ_rows,
        weight.reshape(9, 3 * width, width), slots,
    )
    scale = float(listed * rows * columns * V) ** (-0.5)
    mine, theirs, grad_in = weight_call(
        neighbours, routes, core, hidden, layers, remote, came, occ_rows, scale, jnp.bfloat16,
        placed[0],
    )
    near, far, back = hold_call(placed[1:], came)
    near, far, back = hop(near, 1), hop(far, 1), hop(back, -1)
    near, far, back, theirs = hold_call([near, far, back, theirs], [mine])
    far = hop(far, 1)

    chip_sum = chip_call(mine, to_other_core(theirs), [far])
    mate = to_other_core(jnp.stack([block[1] for block in (placed[0], near, far, back)]))
    owned_out = collect_call(from_place, placed[0], near, far, back, mate)
    same_core = [
        [(2 * layer + core_id) * columns + q for q in range(columns) for layer in range(depth)]
        for core_id in range(2)
    ]

    def all_to_all(pieces):
        return lax.all_to_all(
            pieces, ("gx", "gy"), 0, 0, axis_index_groups=same_core, tiled=True
        )

    parts = all_to_all(chip_sum.reshape(columns * depth, -1, width // 2))
    grad, *sends = data_call(neighbours, grad_in, occ_rows, weight, chip_sum)
    landed = [
        from_behind(sends[1], "gx", 1),
        from_behind(sends[0], "gx", -1),
        from_behind(sends[3], "gy", 1),
        from_behind(sends[2], "gy", -1),
    ]
    arrived = [landed[1], landed[0], landed[3], landed[2]]

    pieces = total_call(parts, columns * depth, [*arrived, mate])
    own = all_to_all(pieces)
    input_grad = finish_call(grad, arrived, features, occ_rows, grad_in, pieces)
    own = hold_call([own], [input_grad, owned_out])[0].reshape(chip_sum.shape)
    weight_grad = join_call(core, own, to_other_core(own), input_grad)
    return (owned_out, input_grad, weight_grad)


def solution(mesh):
    return jax.shard_map(
        body,
        mesh=mesh,
        in_specs=(
            P(("gx", "gy"), None, None),
            P(("gx", "gy"), None),
            P(("gx", "gy"), None),
            P(("gx", "gy"), None),
            P(),
            P(("gx", "gy"), None, None),
        ),
        out_specs=(P(("gx", "gy"), None, None), P(("gx", "gy"), None, None), P()),
        check_vma=False,
    )
```

```python
import jax
import jax.numpy as jnp
from jax import lax
from jax.experimental import pallas as pl
from jax.experimental.pallas import tpu as pltpu
from jax.sharding import PartitionSpec as P

EDGE = 8
TAPS = 27
V = 512
FACE = 64
PLANE = 80
MIB = 1 << 20

norm_eps = 1e-06


def from_behind(block, axis, distance):
    count = lax.axis_size(axis)
    return lax.ppermute(block, axis, [(i, (i + distance) % count) for i in range(count)])


def inner_neighbours(neighbours, listed):
    p, q = lax.axis_index("gx"), lax.axis_index("gy")
    inside = jnp.stack(
        [p > 0, p < lax.axis_size("gx") - 1, q > 0, q < lax.axis_size("gy") - 1, True, True]
    )
    return jnp.where(inside[None, :] | (neighbours < listed), neighbours, 2 * listed)


def hop(blocks, sign):
    count = lax.axis_size("gx")
    ways = [
        (p, (p // 2 + (sign if p % 2 == 0 else -sign)) * 2 % count + p % 2)
        for p in range(count)
    ]
    return lax.ppermute(blocks, "gx", ways)


def to_other_core(block):
    return lax.ppermute(block, "gx", [(p, p ^ 1) for p in range(lax.axis_size("gx"))])


def params(limit):
    return pltpu.CompilerParams(vmem_limit_bytes=limit * MIB)


def whole(shape):
    zeros = (0,) * len(shape)
    return pl.BlockSpec(shape, lambda *_: zeros)


def by_brick(shape):
    zeros = (0,) * len(shape)
    return pl.BlockSpec((1,) + shape, lambda s, *_: (s,) + zeros)


def smem():
    return pl.BlockSpec(memory_space=pltpu.SMEM)


def anywhere():
    return pl.BlockSpec(memory_space=pl.ANY)


def glance(arrays):
    specs = []
    for array in arrays:
        zeros = (0,) * array.ndim
        block = (1,) * (array.ndim - 2) + (16, 128)
        specs.append(pl.BlockSpec(block, lambda *_, zeros=zeros: zeros))
    return specs


def mask_of(occ_row, width):
    spread = jnp.broadcast_to(occ_row.astype(jnp.float32), (128, V))
    column = jnp.transpose(spread)
    return jnp.concatenate([column] * (width // 128), axis=1)


def norm_scale(values):
    return lax.rsqrt(jnp.mean(values * values, axis=-1, keepdims=True) + norm_eps)


def sigmoid(u):
    return 1.0 / (1.0 + jnp.exp(-u))


def hidden_kernel(feat_ref, occ_ref, hid_ref, x0_ref, x1_ref, y0_ref, y1_ref):
    width = feat_ref.shape[2]
    values = feat_ref[0].astype(jnp.float32)
    u = values * norm_scale(values)
    hidden = mask_of(occ_ref[0], width) * (u * sigmoid(u))
    hid_ref[0] = hidden.astype(jnp.bfloat16)
    cube = hidden.reshape(EDGE, EDGE, EDGE, width)
    x0_ref[0] = cube[0].reshape(FACE, width).astype(jnp.bfloat16)
    x1_ref[0] = cube[EDGE - 1].reshape(FACE, width).astype(jnp.bfloat16)
    y0_ref[0] = cube[:, 0].reshape(FACE, width).astype(jnp.bfloat16)
    y1_ref[0] = cube[:, EDGE - 1].reshape(FACE, width).astype(jnp.bfloat16)


def hidden_call(features, occ_rows):
    listed, _, width = features.shape
    layer = jax.ShapeDtypeStruct((listed, FACE, width), jnp.bfloat16)
    return pl.pallas_call(
        hidden_kernel,
        grid=(listed,),
        in_specs=[by_brick((V, width)), by_brick((1, V))],
        out_specs=[by_brick((V, width))] + [by_brick((FACE, width))] * 4,
        out_shape=[jax.ShapeDtypeStruct((listed, V, width), jnp.bfloat16)] + [layer] * 4,
        compiler_params=params(56),
        name="hidden",
    )(features, occ_rows)


def hold_kernel(*refs):
    pass


def hold_call(blocks, after):
    return pl.pallas_call(
        hold_kernel,
        grid=(1,),
        in_specs=[anywhere()] * len(blocks) + glance(after),
        out_specs=[anywhere()] * len(blocks),
        out_shape=[jax.ShapeDtypeStruct(block.shape, block.dtype) for block in blocks],
        input_output_aliases={i: i for i in range(len(blocks))},
        compiler_params=params(16),
        name="hold",
    )(*blocks, *after)


def cut_kernel(blocks_ref, *refs):
    refs[-1][...] = blocks_ref[...]


def cut_call(blocks, part, parts, after):
    count, rows, width = blocks.shape
    shape = (count, rows // parts, width)
    return pl.pallas_call(
        cut_kernel,
        grid=(count // 2,),
        in_specs=[pl.BlockSpec((2,) + shape[1:], lambda i: (i, part, 0))] + glance(after),
        out_specs=pl.BlockSpec((2,) + shape[1:], lambda i: (i, 0, 0)),
        out_shape=jax.ShapeDtypeStruct(shape, blocks.dtype),
        compiler_params=params(56),
        name="cut",
    )(blocks, *after)


def collect_kernel(
    place_ref, own_ref, near_ref, far_ref, back_ref, mate_ref, after_ref, out_ref
):
    for step, came_ref in enumerate((own_ref, near_ref, far_ref, back_ref)):
        out_ref[place_ref[2 * step]] = came_ref[0]
        out_ref[place_ref[2 * step + 1]] = mate_ref[step]


def collect_call(place, own, near, far, back, mate, after):
    shape = (2 * mate.shape[0],) + mate.shape[1:]
    return pl.pallas_call(
        collect_kernel,
        grid=(1,),
        in_specs=[smem()] + [whole(own.shape)] * 4 + [whole(mate.shape)] + glance([after]),
        out_specs=whole(shape),
        out_shape=jax.ShapeDtypeStruct(shape, mate.dtype),
        compiler_params=params(56),
        cost_estimate=pl.CostEstimate(
            flops=0, bytes_accessed=4 * shape[0] * shape[1] * shape[2], transcendentals=0
        ),
        name="collect",
    )(place, own, near, far, back, mate, after)


def roll_c(block, shift):
    flat = block.reshape((-1,) + block.shape[-2:])
    return pltpu.roll(flat, shift % EDGE, 1).reshape(block.shape)


def c_index(shape):
    return lax.broadcasted_iota(jnp.int32, shape, len(shape) - 2)


def extended_brick(s, near_ref, hid_ref, own, far, store):
    listed, _, width = hid_ref.shape

    def flag(condition):
        return jnp.where(condition, 1.0, 0.0).astype(jnp.float32)

    def face(f):
        n = near_ref[s, f]
        here = own[f ^ 1][jnp.minimum(n, listed - 1)].astype(jnp.float32)
        there = far[f][jnp.clip(n - listed, 0, listed - 1)].astype(jnp.float32)
        value = here * flag(n < listed) + there * flag((n >= listed) & (n < 2 * listed))
        return value.reshape(EDGE, EDGE, width)

    def column(f):
        n = near_ref[s, f]
        brick = hid_ref[jnp.minimum(n, listed - 1)].astype(jnp.float32) * flag(n < listed)
        return brick.reshape(EDGE, EDGE, EDGE, width)

    def extended(core, sides):
        x0, x1, y0, y1 = sides
        blank = jnp.zeros((1, EDGE, width), jnp.float32)
        middle = jnp.concatenate([y0[:, None], core, y1[:, None]], axis=1)
        first = jnp.concatenate([blank, x0, blank], axis=0)[None]
        last = jnp.concatenate([blank, x1, blank], axis=0)[None]
        return jnp.concatenate([first, middle, last], axis=0)

    def put(k, block):
        everything = block.reshape(EDGE + 2, PLANE, width).astype(jnp.bfloat16)
        inner = block[:, 1 : EDGE + 1].reshape(EDGE + 2, FACE, width).astype(jnp.bfloat16)
        store(k, everything, inner)

    core = hid_ref[s].astype(jnp.float32).reshape(EDGE, EDGE, EDGE, width)
    sides = [face(f) for f in range(4)]
    at = c_index(core.shape)
    at_side = c_index(sides[0].shape)
    for k, edge, f in ((0, EDGE - 1, 4), (2, 0, 5)):
        shown = extended(
            jnp.where(at == edge, column(f), core),
            [jnp.where(at_side == edge, 0.0, side) for side in sides],
        )
        put(k, roll_c(shown, 1 - k))
    put(1, extended(core, sides))


def window(even_ref, odd_ref, s, i, j, k):
    if j == 1:
        part = odd_ref[s, k, pl.ds(i, EDGE)]
    else:
        part = even_ref[s, k, pl.ds(i, EDGE), j * EDGE : j * EDGE + FACE]
    return part.reshape(V, part.shape[-1])


def forward_kernel(
    near_ref, place_ref, hid_ref, l0, l1, l2, l3, r0, r1, r2, r3, feat_ref, occ_ref, w_ref,
    *refs,
):
    outs, even_ref, odd_ref = refs[:-2], refs[-2], refs[-1]
    s = pl.program_id(0)
    width = feat_ref.shape[2]

    @pl.when(s == 0)
    def _():
        for out_ref in outs:
            out_ref[...] = jnp.zeros_like(out_ref)

    def store(k, everything, inner):
        even_ref[0, k] = everything
        odd_ref[0, k] = inner

    extended_brick(s, near_ref, hid_ref, (l0, l1, l2, l3), (r0, r1, r2, r3), store)
    total = jnp.zeros((V, width), jnp.float32)
    for i in range(3):
        for j in range(3):
            rows = jnp.concatenate(
                [window(even_ref, odd_ref, 0, i, j, k) for k in range(3)], axis=1
            )
            total = total + jnp.dot(rows, w_ref[3 * i + j], preferred_element_type=jnp.float32)
    result = feat_ref[0].astype(jnp.float32) + mask_of(occ_ref[0], width) * total
    result = result.astype(jnp.bfloat16)
    for step, out_ref in enumerate(outs):

        @pl.when(place_ref[s] // 2 == step)
        def _():
            out_ref[place_ref[s] % 2] = result


def extended_scratch(bricks, width):
    return [
        pltpu.VMEM((bricks, 3, EDGE + 2, PLANE, width), jnp.bfloat16),
        pltpu.VMEM((bricks, 3, EDGE + 2, FACE, width), jnp.bfloat16),
    ]


def forward_call(neighbours, place, hidden, layers, remote, features, occ_rows, weight9, slots):
    listed, _, width = features.shape
    layer = whole((listed, FACE, width))
    return pl.pallas_call(
        forward_kernel,
        grid=(listed,),
        in_specs=[smem(), smem(), whole((listed, V, width))]
        + [layer] * 8
        + [by_brick((V, width)), by_brick((1, V)), whole(weight9.shape)],
        out_specs=[whole((2, V, width))] * (slots // 2),
        out_shape=[jax.ShapeDtypeStruct((2, V, width), jnp.bfloat16)] * (slots // 2),
        scratch_shapes=extended_scratch(1, width),
        compiler_params=params(56),
        cost_estimate=pl.CostEstimate(
            flops=2 * listed * V * TAPS * width * width,
            bytes_accessed=10 * MIB,
            transcendentals=0,
        ),
        name="forward",
    )(neighbours, place, hidden, *layers, *remote, features, occ_rows, weight9)


def weight_kernel(
    near_ref, place_ref, core_ref, hid_ref, l0, l1, l2, l3, r0, r1, r2, r3, occ_ref, after_ref,
    *refs, scale,
):
    came, refs = refs[:-7], refs[-7:]
    mine_ref, theirs_ref, grad_ref, even_ref, odd_ref, turned_ref, sem = refs
    part = V // len(came)
    i = pl.program_id(0)
    listed, _, width = hid_ref.shape
    half = width // 2

    def copy(t, s):
        return pltpu.make_async_copy(
            came[t].at[place_ref[s, 0]],
            grad_ref.at[s, pl.ds(t * part, part)],
            sem.at[t * listed + s],
        )

    @pl.when(i == 0)
    def _():
        for s in range(listed):
            for t in range(len(came)):
                copy(t, s).start()

        @pl.loop(0, listed)
        def _(s):
            def store(k, everything, inner):
                even_ref[s, k] = everything
                odd_ref[s, k] = inner

            extended_brick(s, near_ref, hid_ref, (l0, l1, l2, l3), (r0, r1, r2, r3), store)

        for s in range(listed):
            for t in range(len(came)):
                copy(t, s).wait()
            mixed = grad_ref[s].astype(jnp.float32) * mask_of(occ_ref[s], width)
            turned_ref[:, s * V : (s + 1) * V] = jnp.transpose(mixed).astype(jnp.bfloat16)

    @pl.when(i < 3)
    def _():
        first = core_ref[0] == 0
        for j in range(3):
            for k in range(3):
                rows = jnp.concatenate(
                    [window(even_ref, odd_ref, s, i, j, k) for s in range(listed)], axis=0
                )
                product = jnp.dot(turned_ref[...], rows, preferred_element_type=jnp.float32)
                product = jnp.transpose(product) * scale
                low, high = product[:, :half], product[:, half:]
                mine_ref[3 * j + k] = jnp.where(first, low, high)
                theirs_ref[3 * j + k] = jnp.where(first, high, low).astype(theirs_ref.dtype)

    @pl.when(i == 3)
    def _():
        mine_ref[...] = jnp.zeros_like(mine_ref)
        theirs_ref[...] = jnp.zeros_like(theirs_ref)


def weight_call(
    neighbours, place, core, hidden, layers, remote, came, occ_rows, scale, kind, after
):
    listed, _, width = hidden.shape
    shape = (TAPS + 1, width, width // 2)
    block = pl.BlockSpec((9, width, width // 2), lambda i: (i, 0, 0))
    return pl.pallas_call(
        lambda *refs: weight_kernel(*refs, scale=scale),
        grid=(4,),
        in_specs=[smem(), smem(), smem(), whole(hidden.shape)]
        + [whole((listed, FACE, width))] * 8
        + [whole(occ_rows.shape)]
        + glance([after])
        + [anywhere()] * len(came),
        out_specs=[block, block, whole(hidden.shape)],
        out_shape=[
            jax.ShapeDtypeStruct(shape, jnp.float32),
            jax.ShapeDtypeStruct(shape, kind),
            jax.ShapeDtypeStruct(hidden.shape, jnp.bfloat16),
        ],
        scratch_shapes=extended_scratch(listed, width)
        + [pltpu.VMEM((width, listed * V), jnp.bfloat16), pltpu.SemaphoreType.DMA((len(came) * listed,))],
        compiler_params=params(32),
        cost_estimate=pl.CostEstimate(
            flops=2 * listed * V * TAPS * width * width,
            bytes_accessed=10 * MIB,
            transcendentals=0,
        ),
        name="weight_gradient",
    )(neighbours, place, core, hidden, *layers, *remote, occ_rows, after, *came)


def chip_kernel(mine_ref, theirs_ref, *refs):
    out_ref = refs[-1]
    added = mine_ref[...] + theirs_ref[...].astype(jnp.float32)
    out_ref[...] = added.astype(jnp.bfloat16)


def chip_call(mine, theirs, after):
    taps, width, half = mine.shape
    block = pl.BlockSpec((7, width, half), lambda t: (t, 0, 0))
    return pl.pallas_call(
        chip_kernel,
        grid=(taps // 7,),
        in_specs=[block, block] + glance(after),
        out_specs=block,
        out_shape=jax.ShapeDtypeStruct(mine.shape, jnp.bfloat16),
        compiler_params=params(12),
        name="chip_sum",
    )(mine, theirs, *after)


def total_kernel(parts_ref, *refs):
    out_ref = refs[-1]
    total = jnp.sum(parts_ref[...].astype(jnp.float32), axis=0)
    for z in range(out_ref.shape[0]):
        out_ref[z] = total.astype(jnp.bfloat16)


def total_call(parts, copies, after):
    _, rows, half = parts.shape
    return pl.pallas_call(
        total_kernel,
        grid=(1,),
        in_specs=[whole(parts.shape)] + glance(after),
        out_specs=whole((copies, rows, half)),
        out_shape=jax.ShapeDtypeStruct((copies, rows, half), jnp.bfloat16),
        compiler_params=params(20),
        name="total",
    )(parts, *after)


def join_kernel(core_ref, own_ref, other_ref, after0_ref, after1_ref, out_ref):
    half = own_ref.shape[2]
    first = core_ref[0] == 0

    def put(low_ref, high_ref):
        out_ref[:, :, :half] = low_ref[...].astype(jnp.float32)
        out_ref[:, :, half:] = high_ref[...].astype(jnp.float32)

    @pl.when(first)
    def _():
        put(own_ref, other_ref)

    @pl.when(jnp.logical_not(first))
    def _():
        put(other_ref, own_ref)


def join_call(core, own, other, after):
    _, width, half = own.shape
    block = pl.BlockSpec((9, width, half), lambda t: (t, 0, 0))
    return pl.pallas_call(
        join_kernel,
        grid=(TAPS // 9,),
        in_specs=[smem(), block, block] + glance(after),
        out_specs=pl.BlockSpec((9, width, 2 * half), lambda t: (t, 0, 0)),
        out_shape=jax.ShapeDtypeStruct((TAPS, width, 2 * half), jnp.float32),
        compiler_params=params(16),
        name="join",
    )(core, own, other, *after)


def data_kernel(
    near_ref, buf_ref, occ_ref, w_ref,
    grad_ref, s0_ref, s1_ref, s2_ref, s3_ref,
    wide_ref, rows_ref, depth_ref, kept_ref,
):
    s = pl.program_id(0)
    listed = grad_ref.shape[0]
    width = buf_ref.shape[2]
    last = s == listed - 1

    mixed = buf_ref[0].astype(jnp.float32) * mask_of(occ_ref[0], width)
    cube = mixed.reshape(FACE, EDGE, width)
    at = c_index(cube.shape)

    def three(block, index):
        ahead = jnp.where(index == EDGE - 1, 0.0, roll_c(block, -1))
        behind = jnp.where(index == 0, 0.0, roll_c(block, 1))
        flat = (-1, width)
        return [entry.reshape(flat).astype(jnp.bfloat16) for entry in (ahead, block, behind)]

    def back(rows, taps):
        return sum(
            lax.dot_general(
                row, w_ref[tap], (((1,), (1,)), ((), ())), preferred_element_type=jnp.float32
            )
            for row, tap in zip(rows, taps)
        )

    rows = three(cube, at)
    wide_ref[...] = jnp.zeros_like(wide_ref)
    for i in range(3):
        for j in range(3):
            product = back(rows, [9 * i + 3 * j + k for k in range(3)])
            wide_ref[i : i + EDGE, j * EDGE : j * EDGE + FACE] += product.reshape(
                EDGE, FACE, width
            )

    def rounded(block):
        return block.astype(jnp.bfloat16).astype(jnp.float32)

    inside = slice(EDGE, EDGE + FACE)
    grad_ref[s] = rounded(wide_ref[1 : EDGE + 1, inside].reshape(V, width))
    kept_ref[s, 0] = rounded(wide_ref[0, inside])
    kept_ref[s, 1] = rounded(wide_ref[EDGE + 1, inside])
    kept_ref[s, 2] = rounded(wide_ref[1 : EDGE + 1, 0:EDGE].reshape(FACE, width))
    kept_ref[s, 3] = rounded(wide_ref[1 : EDGE + 1, PLANE - EDGE : PLANE].reshape(FACE, width))

    halves = range(width // 128)
    for half in halves:
        rows_ref[half] = mixed[:, half * 128 : (half + 1) * 128]
    for side, c in ((0, 0), (1, EDGE - 1)):
        layer = jnp.concatenate(
            [rows_ref[half, pl.ds(c, FACE, stride=EDGE)] for half in halves], axis=1
        )
        layer = layer.reshape(EDGE, EDGE, width)
        for j, entry in enumerate(three(layer, c_index(layer.shape))):
            depth_ref[side, j, pl.ds(s * FACE, FACE)] = entry

    @pl.when(last)
    def _():
        sends = (s0_ref, s1_ref, s2_ref, s3_ref)
        for side in range(2):
            total = jnp.zeros((listed, EDGE + 2, EDGE, width), jnp.float32)
            for i in range(3):
                product = back(
                    [depth_ref[side, j] for j in range(3)],
                    [9 * i + 3 * j + 2 * side for j in range(3)],
                ).reshape(listed, EDGE, EDGE, width)
                pieces = [product]
                if i > 0:
                    pieces.insert(0, jnp.zeros((listed, i, EDGE, width), jnp.float32))
                if i < 2:
                    pieces.append(jnp.zeros((listed, 2 - i, EDGE, width), jnp.float32))
                total = total + jnp.concatenate(pieces, axis=1)
            rows_ref[...] = jnp.zeros_like(rows_ref)
            for h in range(listed):
                n = near_ref[h, 4 + side]

                @pl.when(n < listed)
                def _():
                    piece = rounded(total[h, 1 : EDGE + 1].reshape(FACE, width))
                    c = (EDGE - 1) * (1 - side)
                    for half in halves:
                        rows_ref[half, pl.ds(c, FACE, stride=EDGE)] = piece[
                            :, half * 128 : (half + 1) * 128
                        ]
                    grad_ref[n] += jnp.concatenate([rows_ref[half] for half in halves], axis=1)

        for f in range(4):
            sums = [jnp.zeros((FACE, width), jnp.float32) for _ in range(listed)]
            for h in range(listed):
                n = near_ref[h, f]
                piece = kept_ref[h, f]
                sums = [
                    total + piece * jnp.where(n == listed + t, 1.0, 0.0).astype(jnp.float32)
                    for t, total in enumerate(sums)
                ]

                @pl.when(n < listed)
                def _():
                    add_face(grad_ref, n, f, piece)

            for t in range(listed):
                sends[f][t] = sums[t].astype(jnp.bfloat16)


def add_face(ref, n, f, piece):
    near_end = f % 2 == 1
    if f < 2:
        start = 0 if near_end else V - FACE
        ref[n, start : start + FACE] += piece
    else:
        for a in range(EDGE):
            start = a * FACE + (0 if near_end else FACE - EDGE)
            ref[n, start : start + EDGE] += piece[a * EDGE : (a + 1) * EDGE]


def data_call(neighbours, grad_in, occ_rows, weight):
    listed, _, width = grad_in.shape
    layer = jax.ShapeDtypeStruct((listed, FACE, width), jnp.bfloat16)
    return pl.pallas_call(
        data_kernel,
        grid=(listed,),
        in_specs=[smem(), by_brick((V, width)), by_brick((1, V)), whole(weight.shape)],
        out_specs=[whole((listed, V, width))] + [whole(layer.shape)] * 4,
        out_shape=[jax.ShapeDtypeStruct((listed, V, width), jnp.float32)] + [layer] * 4,
        scratch_shapes=[
            pltpu.VMEM((EDGE + 2, PLANE, width), jnp.float32),
            pltpu.VMEM((width // 128, V, 128), jnp.float32),
            pltpu.VMEM((2, 3, listed * FACE, width), jnp.bfloat16),
            pltpu.VMEM((listed, 4, FACE, width), jnp.float32),
        ],
        compiler_params=params(32),
        cost_estimate=pl.CostEstimate(
            flops=2 * listed * V * (TAPS + 3) * width * width,
            bytes_accessed=10 * MIB,
            transcendentals=0,
        ),
        name="data_gradient",
    )(neighbours, grad_in, occ_rows, weight)


def finish_kernel(
    grad_ref, r0, r1, r2, r3, feat_ref, occ_ref, buf_ref, after_ref, out_ref, work_ref
):
    width = feat_ref.shape[2]
    work_ref[...] = grad_ref[...]
    for f, far in enumerate((r0, r1, r2, r3)):
        add_face(work_ref, 0, f, far[0].astype(jnp.float32))
    values = feat_ref[0].astype(jnp.float32)
    r = norm_scale(values)
    u = values * r
    sig = sigmoid(u)
    d_u = mask_of(occ_ref[0], width) * work_ref[0] * (sig * (1.0 + u * (1.0 - sig)))
    pulled = r * (d_u - u * jnp.mean(u * d_u, axis=-1, keepdims=True))
    out_ref[0] = (buf_ref[0].astype(jnp.float32) + pulled).astype(jnp.bfloat16)


def finish_call(grad, remote, features, occ_rows, grad_in, after):
    listed, _, width = features.shape
    return pl.pallas_call(
        finish_kernel,
        grid=(listed,),
        in_specs=[by_brick((V, width))]
        + [by_brick((FACE, width))] * 4
        + [by_brick((V, width)), by_brick((1, V)), by_brick((V, width))]
        + glance([after]),
        out_specs=by_brick((V, width)),
        out_shape=jax.ShapeDtypeStruct((listed, V, width), jnp.bfloat16),
        scratch_shapes=[pltpu.VMEM((1, V, width), jnp.float32)],
        compiler_params=params(56),
        cost_estimate=pl.CostEstimate(
            flops=0, bytes_accessed=10 * listed * V * width, transcendentals=listed * V * width
        ),
        name="input_gradient",
    )(grad, *remote, features, occ_rows, grad_in, after)


def body(features, occupancy, routes, neighbours, weight, cotangent):
    listed, _, width = features.shape
    slots = cotangent.shape[0]
    rows, columns = lax.axis_size("gx"), lax.axis_size("gy")
    depth = rows // 2
    p = lax.axis_index("gx").astype(jnp.int32)
    z, c = p // 2, p % 2
    core = c.reshape(1)
    occ_rows = occupancy.reshape(listed, 1, V)
    neighbours = inner_neighbours(neighbours, listed)
    steps = jnp.arange(slots, dtype=jnp.int32)
    def way_of(core_id):
        return 1 - 2 * core_id

    source_core = (c + steps) % 2
    from_place = (z - way_of(source_core) * (steps // 2)) % depth * 2 + source_core
    route = routes[:, 0]
    out_place = way_of(c) * (route // 2 - z) % depth * 2 + (route + c) % 2

    hidden, *layers = hidden_call(features, occ_rows)
    remote = [
        from_behind(layers[1], "gx", 1),
        from_behind(layers[0], "gx", -1),
        from_behind(layers[3], "gy", 1),
        from_behind(layers[2], "gy", -1),
    ]
    came = [
        lax.all_to_all(cut_call(cotangent, part, 2, after), "gx", 0, 0, tiled=True)
        for part, after in ((0, []), (1, remote[:2]))
    ]
    placed = forward_call(
        neighbours, out_place, hidden, layers, remote, features, occ_rows,
        weight.reshape(9, 3 * width, width), slots,
    )
    scale = float(listed * rows * columns * V) ** (-0.5)
    mine, theirs, grad_in = weight_call(
        neighbours, routes, core, hidden, layers, remote, came, occ_rows, scale, jnp.bfloat16,
        placed[0],
    )
    near, far, back = hold_call(placed[1:], came)
    near, far, back = hop(near, 1), hop(far, 1), hop(back, -1)
    near, far, back, theirs = hold_call([near, far, back, theirs], [mine])
    far = hop(far, 1)

    grad, *sends = data_call(neighbours, grad_in, occ_rows, weight)

    chip_sum = chip_call(mine, to_other_core(theirs), [far, grad])
    mate = to_other_core(jnp.stack([block[1] for block in (placed[0], near, far, back)]))
    same_core = [
        [(2 * layer + core_id) * columns + q for q in range(columns) for layer in range(depth)]
        for core_id in range(2)
    ]

    def all_to_all(pieces):
        return lax.all_to_all(
            pieces, ("gx", "gy"), 0, 0, axis_index_groups=same_core, tiled=True
        )

    parts = all_to_all(chip_sum.reshape(columns * depth, -1, width // 2))
    landed = [
        from_behind(sends[1], "gx", 1),
        from_behind(sends[0], "gx", -1),
        from_behind(sends[3], "gy", 1),
        from_behind(sends[2], "gy", -1),
    ]
    arrived = [landed[1], landed[0], landed[3], landed[2]]

    pieces = total_call(parts, columns * depth, [*arrived, mate])
    own = all_to_all(pieces).reshape(chip_sum.shape)
    owned_out = collect_call(from_place, placed[0], near, far, back, mate, pieces)
    input_grad = finish_call(grad, arrived, features, occ_rows, grad_in, pieces)
    weight_grad = join_call(core, own, to_other_core(own), [owned_out, input_grad])
    return (owned_out, input_grad, weight_grad)


def solution(mesh):
    return jax.shard_map(
        body,
        mesh=mesh,
        in_specs=(
            P(("gx", "gy"), None, None),
            P(("gx", "gy"), None),
            P(("gx", "gy"), None),
            P(("gx", "gy"), None),
            P(),
            P(("gx", "gy"), None, None),
        ),
        out_specs=(P(("gx", "gy"), None, None), P(("gx", "gy"), None, None), P()),
        check_vma=False,
    )
```

```python
import jax
import jax.numpy as jnp
from jax import lax
from jax.experimental import pallas as pl
from jax.experimental.pallas import tpu as pltpu
from jax.sharding import PartitionSpec as P

EDGE = 8
TAPS = 27
V = 512
FACE = 64
PLANE = 80
MIB = 1 << 20

norm_eps = 1e-06


def from_behind(block, distance):
    count = lax.axis_size("gx")
    return lax.ppermute(block, "gx", [(i, (i + distance) % count) for i in range(count)])


def column_pair(first, second):
    rows, columns = lax.axis_size("gx"), lax.axis_size("gy")

    def shifted(block, sign):
        ways = []
        for p in range(rows):
            step = sign if p % 2 == 0 else -sign
            ways += [(p * columns + q, p * columns + (q + step) % columns) for q in range(columns)]
        return lax.ppermute(block, ("gx", "gy"), ways)

    return shifted(first, 1), shifted(second, -1)


def inner_neighbours(neighbours, listed):
    p, q = lax.axis_index("gx"), lax.axis_index("gy")
    inside = jnp.stack(
        [p > 0, p < lax.axis_size("gx") - 1, q > 0, q < lax.axis_size("gy") - 1, True, True]
    )
    return jnp.where(inside[None, :] | (neighbours < listed), neighbours, 2 * listed)


def hop(blocks, sign):
    count = lax.axis_size("gx")
    ways = [
        (p, (p // 2 + (sign if p % 2 == 0 else -sign)) * 2 % count + p % 2)
        for p in range(count)
    ]
    return lax.ppermute(blocks, "gx", ways)


def to_other_core(block):
    return lax.ppermute(block, "gx", [(p, p ^ 1) for p in range(lax.axis_size("gx"))])


def params(limit):
    return pltpu.CompilerParams(vmem_limit_bytes=limit * MIB)


def whole(shape):
    zeros = (0,) * len(shape)
    return pl.BlockSpec(shape, lambda *_: zeros)


def by_brick(shape):
    zeros = (0,) * len(shape)
    return pl.BlockSpec((1,) + shape, lambda s, *_: (s,) + zeros)


def smem():
    return pl.BlockSpec(memory_space=pltpu.SMEM)


def anywhere():
    return pl.BlockSpec(memory_space=pl.ANY)


def glance(arrays):
    specs = []
    for array in arrays:
        zeros = (0,) * array.ndim
        block = (1,) * (array.ndim - 2) + (16, 128)
        specs.append(pl.BlockSpec(block, lambda *_, zeros=zeros: zeros))
    return specs


def mask_of(occ_row, width):
    spread = jnp.broadcast_to(occ_row.astype(jnp.float32), (128, V))
    column = jnp.transpose(spread)
    return jnp.concatenate([column] * (width // 128), axis=1)


def norm_scale(values):
    return lax.rsqrt(jnp.mean(values * values, axis=-1, keepdims=True) + norm_eps)


def sigmoid(u):
    return 1.0 / (1.0 + jnp.exp(-u))


def hidden_kernel(core_ref, feat_ref, occ_ref, hid_ref, x0_ref, x1_ref, ya_ref, yb_ref):
    width = feat_ref.shape[2]
    values = feat_ref[0].astype(jnp.float32)
    u = values * norm_scale(values)
    hidden = mask_of(occ_ref[0], width) * (u * sigmoid(u))
    hid_ref[0] = hidden.astype(jnp.bfloat16)
    cube = hidden.reshape(EDGE, EDGE, EDGE, width)
    x0_ref[0] = cube[0].reshape(FACE, width).astype(jnp.bfloat16)
    x1_ref[0] = cube[EDGE - 1].reshape(FACE, width).astype(jnp.bfloat16)
    first = core_ref[0] == 0
    low, high = cube[:, 0].reshape(FACE, width), cube[:, EDGE - 1].reshape(FACE, width)
    ya_ref[0] = jnp.where(first, high, low).astype(jnp.bfloat16)
    yb_ref[0] = jnp.where(first, low, high).astype(jnp.bfloat16)


def hidden_call(core, features, occ_rows):
    listed, _, width = features.shape
    layer = jax.ShapeDtypeStruct((listed, FACE, width), jnp.bfloat16)
    return pl.pallas_call(
        hidden_kernel,
        grid=(listed,),
        in_specs=[smem(), by_brick((V, width)), by_brick((1, V))],
        out_specs=[by_brick((V, width))] + [by_brick((FACE, width))] * 4,
        out_shape=[jax.ShapeDtypeStruct((listed, V, width), jnp.bfloat16)] + [layer] * 4,
        compiler_params=params(16),
        name="hidden",
    )(core, features, occ_rows)


def hold_kernel(*refs):
    pass


def hold_call(blocks, after):
    return pl.pallas_call(
        hold_kernel,
        grid=(1,),
        in_specs=[anywhere()] * len(blocks) + glance(after),
        out_specs=[anywhere()] * len(blocks),
        out_shape=[jax.ShapeDtypeStruct(block.shape, block.dtype) for block in blocks],
        input_output_aliases={i: i for i in range(len(blocks))},
        compiler_params=params(16),
        name="hold",
    )(*blocks, *after)


def collect_kernel(
    place_ref, own_ref, near_ref, far_ref, back_ref, mate_ref, after_ref, out_ref
):
    for step, came_ref in enumerate((own_ref, near_ref, far_ref, back_ref)):
        out_ref[place_ref[2 * step]] = came_ref[0]
        out_ref[place_ref[2 * step + 1]] = mate_ref[step]


def collect_call(place, own, near, far, back, mate, after):
    shape = (2 * mate.shape[0],) + mate.shape[1:]
    return pl.pallas_call(
        collect_kernel,
        grid=(1,),
        in_specs=[smem()] + [whole(own.shape)] * 4 + [whole(mate.shape)] + glance([after]),
        out_specs=whole(shape),
        out_shape=jax.ShapeDtypeStruct(shape, mate.dtype),
        compiler_params=params(20),
        cost_estimate=pl.CostEstimate(
            flops=0, bytes_accessed=4 * shape[0] * shape[1] * shape[2], transcendentals=0
        ),
        name="collect",
    )(place, own, near, far, back, mate, after)


def roll_c(block, shift):
    flat = block.reshape((-1,) + block.shape[-2:])
    return pltpu.roll(flat, shift % EDGE, 1).reshape(block.shape)


def c_index(shape):
    return lax.broadcasted_iota(jnp.int32, shape, len(shape) - 2)


def extended_brick(s, near_ref, core_ref, hid_ref, own, far, store):
    listed, _, width = hid_ref.shape

    def flag(condition):
        return jnp.where(condition, 1.0, 0.0).astype(jnp.float32)

    first = core_ref[0] == 0

    def face(f):
        n = near_ref[s, f]
        at_here, at_there = jnp.minimum(n, listed - 1), jnp.clip(n - listed, 0, listed - 1)
        if f < 2:
            here, there = own[f ^ 1][at_here], far[f][at_there]
        else:
            a, b = (2, 3) if f == 2 else (3, 2)
            here = jnp.where(first, own[a][at_here], own[b][at_here])
            there = jnp.where(first, far[a][at_there], far[b][at_there])
        here, there = here.astype(jnp.float32), there.astype(jnp.float32)
        value = here * flag(n < listed) + there * flag((n >= listed) & (n < 2 * listed))
        return value.reshape(EDGE, EDGE, width)

    def column(f):
        n = near_ref[s, f]
        brick = hid_ref[jnp.minimum(n, listed - 1)].astype(jnp.float32) * flag(n < listed)
        return brick.reshape(EDGE, EDGE, EDGE, width)

    def extended(core, sides):
        x0, x1, y0, y1 = sides
        blank = jnp.zeros((1, EDGE, width), jnp.float32)
        middle = jnp.concatenate([y0[:, None], core, y1[:, None]], axis=1)
        first = jnp.concatenate([blank, x0, blank], axis=0)[None]
        last = jnp.concatenate([blank, x1, blank], axis=0)[None]
        return jnp.concatenate([first, middle, last], axis=0)

    def put(k, block):
        everything = block.reshape(EDGE + 2, PLANE, width).astype(jnp.bfloat16)
        inner = block[:, 1 : EDGE + 1].reshape(EDGE + 2, FACE, width).astype(jnp.bfloat16)
        store(k, everything, inner)

    core = hid_ref[s].astype(jnp.float32).reshape(EDGE, EDGE, EDGE, width)
    sides = [face(f) for f in range(4)]
    at = c_index(core.shape)
    at_side = c_index(sides[0].shape)
    for k, edge, f in ((0, EDGE - 1, 4), (2, 0, 5)):
        shown = extended(
            jnp.where(at == edge, column(f), core),
            [jnp.where(at_side == edge, 0.0, side) for side in sides],
        )
        put(k, roll_c(shown, 1 - k))
    put(1, extended(core, sides))


def window(even_ref, odd_ref, s, i, j, k):
    if j == 1:
        part = odd_ref[s, k, pl.ds(i, EDGE)]
    else:
        part = even_ref[s, k, pl.ds(i, EDGE), j * EDGE : j * EDGE + FACE]
    return part.reshape(V, part.shape[-1])


def forward_kernel(
    near_ref, place_ref, core_ref, hid_ref, l0, l1, l2, l3, r0, r1, r2, r3, feat_ref, occ_ref, w_ref,
    *refs,
):
    outs, even_ref, odd_ref = refs[:-2], refs[-2], refs[-1]
    s = pl.program_id(0)
    width = feat_ref.shape[2]

    @pl.when(s == 0)
    def _():
        for out_ref in outs:
            out_ref[...] = jnp.zeros_like(out_ref)

    def store(k, everything, inner):
        even_ref[0, k] = everything
        odd_ref[0, k] = inner

    extended_brick(s, near_ref, core_ref, hid_ref, (l0, l1, l2, l3), (r0, r1, r2, r3), store)
    total = jnp.zeros((V, width), jnp.float32)
    for i in range(3):
        for j in range(3):
            rows = jnp.concatenate(
                [window(even_ref, odd_ref, 0, i, j, k) for k in range(3)], axis=1
            )
            total = total + jnp.dot(rows, w_ref[3 * i + j], preferred_element_type=jnp.float32)
    result = feat_ref[0].astype(jnp.float32) + mask_of(occ_ref[0], width) * total
    result = result.astype(jnp.bfloat16)
    for step, out_ref in enumerate(outs):

        @pl.when(place_ref[s] // 2 == step)
        def _():
            out_ref[place_ref[s] % 2] = result


def extended_scratch(bricks, width):
    return [
        pltpu.VMEM((bricks, 3, EDGE + 2, PLANE, width), jnp.bfloat16),
        pltpu.VMEM((bricks, 3, EDGE + 2, FACE, width), jnp.bfloat16),
    ]


def forward_call(
    neighbours, place, core, hidden, layers, remote, features, occ_rows, weight9, slots
):
    listed, _, width = features.shape
    layer = whole((listed, FACE, width))
    return pl.pallas_call(
        forward_kernel,
        grid=(listed,),
        in_specs=[smem(), smem(), smem(), whole((listed, V, width))]
        + [layer] * 8
        + [by_brick((V, width)), by_brick((1, V)), whole(weight9.shape)],
        out_specs=[whole((2, V, width))] * (slots // 2),
        out_shape=[jax.ShapeDtypeStruct((2, V, width), jnp.bfloat16)] * (slots // 2),
        scratch_shapes=extended_scratch(1, width),
        compiler_params=params(56),
        cost_estimate=pl.CostEstimate(
            flops=2 * listed * V * TAPS * width * width,
            bytes_accessed=10 * MIB,
            transcendentals=0,
        ),
        name="forward",
    )(neighbours, place, core, hidden, *layers, *remote, features, occ_rows, weight9)


def weight_kernel(
    near_ref, place_ref, core_ref, hid_ref, l0, l1, l2, l3, r0, r1, r2, r3, occ_ref, after_ref,
    *refs, scale,
):
    came, refs = refs[:-7], refs[-7:]
    mine_ref, theirs_ref, grad_ref, even_ref, odd_ref, turned_ref, sem = refs
    part = V // len(came)
    i = pl.program_id(0)
    listed, _, width = hid_ref.shape
    half = width // 2

    def copy(t, s):
        return pltpu.make_async_copy(
            came[t].at[place_ref[s, 0]],
            grad_ref.at[s, pl.ds(t * part, part)],
            sem.at[t * listed + s],
        )

    @pl.when(i == 0)
    def _():
        for s in range(listed):
            for t in range(len(came)):
                copy(t, s).start()

        @pl.loop(0, listed)
        def _(s):
            def store(k, everything, inner):
                even_ref[s, k] = everything
                odd_ref[s, k] = inner

            extended_brick(s, near_ref, core_ref, hid_ref, (l0, l1, l2, l3), (r0, r1, r2, r3), store)

        for s in range(listed):
            for t in range(len(came)):
                copy(t, s).wait()
            mixed = grad_ref[s].astype(jnp.float32) * mask_of(occ_ref[s], width)
            turned_ref[:, s * V : (s + 1) * V] = jnp.transpose(mixed).astype(jnp.bfloat16)

    @pl.when(i < 3)
    def _():
        first = core_ref[0] == 0
        for j in range(3):
            for k in range(3):
                rows = jnp.concatenate(
                    [window(even_ref, odd_ref, s, i, j, k) for s in range(listed)], axis=0
                )
                product = jnp.dot(turned_ref[...], rows, preferred_element_type=jnp.float32)
                product = jnp.transpose(product) * scale
                low, high = product[:, :half], product[:, half:]
                mine_ref[3 * j + k] = jnp.where(first, low, high)
                theirs_ref[3 * j + k] = jnp.where(first, high, low).astype(theirs_ref.dtype)

    @pl.when(i == 3)
    def _():
        mine_ref[...] = jnp.zeros_like(mine_ref)
        theirs_ref[...] = jnp.zeros_like(theirs_ref)


def weight_call(
    neighbours, place, core, hidden, layers, remote, came, occ_rows, scale, kind, after
):
    listed, _, width = hidden.shape
    shape = (TAPS + 1, width, width // 2)
    block = pl.BlockSpec((9, width, width // 2), lambda i: (i, 0, 0))
    return pl.pallas_call(
        lambda *refs: weight_kernel(*refs, scale=scale),
        grid=(4,),
        in_specs=[smem(), smem(), smem(), whole(hidden.shape)]
        + [whole((listed, FACE, width))] * 8
        + [whole(occ_rows.shape)]
        + glance([after])
        + [anywhere()] * len(came),
        out_specs=[block, block, whole(hidden.shape)],
        out_shape=[
            jax.ShapeDtypeStruct(shape, jnp.float32),
            jax.ShapeDtypeStruct(shape, kind),
            jax.ShapeDtypeStruct(hidden.shape, jnp.bfloat16),
        ],
        scratch_shapes=extended_scratch(listed, width)
        + [pltpu.VMEM((width, listed * V), jnp.bfloat16), pltpu.SemaphoreType.DMA((len(came) * listed,))],
        compiler_params=params(32),
        cost_estimate=pl.CostEstimate(
            flops=2 * listed * V * TAPS * width * width,
            bytes_accessed=10 * MIB,
            transcendentals=0,
        ),
        name="weight_gradient",
    )(neighbours, place, core, hidden, *layers, *remote, occ_rows, after, *came)


def chip_kernel(mine_ref, theirs_ref, *refs):
    out_ref = refs[-1]
    added = mine_ref[...] + theirs_ref[...].astype(jnp.float32)
    out_ref[...] = added.astype(jnp.bfloat16)


def chip_call(mine, theirs, after):
    taps, width, half = mine.shape
    block = pl.BlockSpec((7, width, half), lambda t: (t, 0, 0))
    return pl.pallas_call(
        chip_kernel,
        grid=(taps // 7,),
        in_specs=[block, block] + glance(after),
        out_specs=block,
        out_shape=jax.ShapeDtypeStruct(mine.shape, jnp.bfloat16),
        compiler_params=params(12),
        name="chip_sum",
    )(mine, theirs, *after)


def total_kernel(parts_ref, *refs):
    out_ref = refs[-1]
    total = jnp.sum(parts_ref[...].astype(jnp.float32), axis=0)
    for z in range(out_ref.shape[0]):
        out_ref[z] = total.astype(jnp.bfloat16)


def total_call(parts, copies, after):
    _, rows, half = parts.shape
    return pl.pallas_call(
        total_kernel,
        grid=(1,),
        in_specs=[whole(parts.shape)] + glance(after),
        out_specs=whole((copies, rows, half)),
        out_shape=jax.ShapeDtypeStruct((copies, rows, half), jnp.bfloat16),
        compiler_params=params(20),
        name="total",
    )(parts, *after)


def join_kernel(core_ref, own_ref, other_ref, after0_ref, after1_ref, out_ref):
    half = own_ref.shape[2]
    first = core_ref[0] == 0

    def put(low_ref, high_ref):
        out_ref[:, :, :half] = low_ref[...].astype(jnp.float32)
        out_ref[:, :, half:] = high_ref[...].astype(jnp.float32)

    @pl.when(first)
    def _():
        put(own_ref, other_ref)

    @pl.when(jnp.logical_not(first))
    def _():
        put(other_ref, own_ref)


def join_call(core, own, other, after):
    _, width, half = own.shape
    block = pl.BlockSpec((9, width, half), lambda t: (t, 0, 0))
    return pl.pallas_call(
        join_kernel,
        grid=(TAPS // 9,),
        in_specs=[smem(), block, block] + glance(after),
        out_specs=pl.BlockSpec((9, width, 2 * half), lambda t: (t, 0, 0)),
        out_shape=jax.ShapeDtypeStruct((TAPS, width, 2 * half), jnp.float32),
        compiler_params=params(16),
        name="join",
    )(core, own, other, *after)


def data_kernel(
    near_ref, core_ref, buf_ref, occ_ref, w_ref,
    grad_ref, s0_ref, s1_ref, sa_ref, sb_ref,
    wide_ref, rows_ref, depth_ref, kept_ref,
):
    s = pl.program_id(0)
    listed = grad_ref.shape[0]
    width = buf_ref.shape[2]
    last = s == listed - 1

    mixed = buf_ref[0].astype(jnp.float32) * mask_of(occ_ref[0], width)
    cube = mixed.reshape(FACE, EDGE, width)
    at = c_index(cube.shape)

    def three(block, index):
        ahead = jnp.where(index == EDGE - 1, 0.0, roll_c(block, -1))
        behind = jnp.where(index == 0, 0.0, roll_c(block, 1))
        flat = (-1, width)
        return [entry.reshape(flat).astype(jnp.bfloat16) for entry in (ahead, block, behind)]

    def back(rows, taps):
        return sum(
            lax.dot_general(
                row, w_ref[tap], (((1,), (1,)), ((), ())), preferred_element_type=jnp.float32
            )
            for row, tap in zip(rows, taps)
        )

    rows = three(cube, at)
    wide_ref[...] = jnp.zeros_like(wide_ref)
    for i in range(3):
        for j in range(3):
            product = back(rows, [9 * i + 3 * j + k for k in range(3)])
            wide_ref[i : i + EDGE, j * EDGE : j * EDGE + FACE] += product.reshape(
                EDGE, FACE, width
            )

    def rounded(block):
        return block.astype(jnp.bfloat16).astype(jnp.float32)

    inside = slice(EDGE, EDGE + FACE)
    grad_ref[s] = rounded(wide_ref[1 : EDGE + 1, inside].reshape(V, width))
    kept_ref[s, 0] = rounded(wide_ref[0, inside])
    kept_ref[s, 1] = rounded(wide_ref[EDGE + 1, inside])
    kept_ref[s, 2] = rounded(wide_ref[1 : EDGE + 1, 0:EDGE].reshape(FACE, width))
    kept_ref[s, 3] = rounded(wide_ref[1 : EDGE + 1, PLANE - EDGE : PLANE].reshape(FACE, width))

    halves = range(width // 128)
    for half in halves:
        rows_ref[half] = mixed[:, half * 128 : (half + 1) * 128]
    for side, c in ((0, 0), (1, EDGE - 1)):
        layer = jnp.concatenate(
            [rows_ref[half, pl.ds(c, FACE, stride=EDGE)] for half in halves], axis=1
        )
        layer = layer.reshape(EDGE, EDGE, width)
        for j, entry in enumerate(three(layer, c_index(layer.shape))):
            depth_ref[side, j, pl.ds(s * FACE, FACE)] = entry

    @pl.when(last)
    def _():
        for side in range(2):
            total = jnp.zeros((listed, EDGE + 2, EDGE, width), jnp.float32)
            for i in range(3):
                product = back(
                    [depth_ref[side, j] for j in range(3)],
                    [9 * i + 3 * j + 2 * side for j in range(3)],
                ).reshape(listed, EDGE, EDGE, width)
                pieces = [product]
                if i > 0:
                    pieces.insert(0, jnp.zeros((listed, i, EDGE, width), jnp.float32))
                if i < 2:
                    pieces.append(jnp.zeros((listed, 2 - i, EDGE, width), jnp.float32))
                total = total + jnp.concatenate(pieces, axis=1)
            rows_ref[...] = jnp.zeros_like(rows_ref)
            for h in range(listed):
                n = near_ref[h, 4 + side]

                @pl.when(n < listed)
                def _():
                    piece = rounded(total[h, 1 : EDGE + 1].reshape(FACE, width))
                    c = (EDGE - 1) * (1 - side)
                    for half in halves:
                        rows_ref[half, pl.ds(c, FACE, stride=EDGE)] = piece[
                            :, half * 128 : (half + 1) * 128
                        ]
                    grad_ref[n] += jnp.concatenate([rows_ref[half] for half in halves], axis=1)

        leaving = []
        for f in range(4):
            sums = [jnp.zeros((FACE, width), jnp.float32) for _ in range(listed)]
            for h in range(listed):
                n = near_ref[h, f]
                piece = kept_ref[h, f]
                sums = [
                    total + piece * jnp.where(n == listed + t, 1.0, 0.0).astype(jnp.float32)
                    for t, total in enumerate(sums)
                ]

                @pl.when(n < listed)
                def _():
                    add_face(grad_ref, n, f, piece)

            leaving.append(sums)
        first = core_ref[0] == 0
        for t in range(listed):
            s0_ref[t] = leaving[0][t].astype(jnp.bfloat16)
            s1_ref[t] = leaving[1][t].astype(jnp.bfloat16)
            sa_ref[t] = jnp.where(first, leaving[3][t], leaving[2][t]).astype(jnp.bfloat16)
            sb_ref[t] = jnp.where(first, leaving[2][t], leaving[3][t]).astype(jnp.bfloat16)


def add_face(ref, n, f, piece):
    near_end = f % 2 == 1
    if f < 2:
        start = 0 if near_end else V - FACE
        ref[n, start : start + FACE] += piece
    else:
        for a in range(EDGE):
            start = a * FACE + (0 if near_end else FACE - EDGE)
            ref[n, start : start + EDGE] += piece[a * EDGE : (a + 1) * EDGE]


def data_call(neighbours, core, grad_in, occ_rows, weight):
    listed, _, width = grad_in.shape
    layer = jax.ShapeDtypeStruct((listed, FACE, width), jnp.bfloat16)
    return pl.pallas_call(
        data_kernel,
        grid=(listed,),
        in_specs=[smem(), smem(), by_brick((V, width)), by_brick((1, V)), whole(weight.shape)],
        out_specs=[whole((listed, V, width))] + [whole(layer.shape)] * 4,
        out_shape=[jax.ShapeDtypeStruct((listed, V, width), jnp.float32)] + [layer] * 4,
        scratch_shapes=[
            pltpu.VMEM((EDGE + 2, PLANE, width), jnp.float32),
            pltpu.VMEM((width // 128, V, 128), jnp.float32),
            pltpu.VMEM((2, 3, listed * FACE, width), jnp.bfloat16),
            pltpu.VMEM((listed, 4, FACE, width), jnp.float32),
        ],
        compiler_params=params(32),
        cost_estimate=pl.CostEstimate(
            flops=2 * listed * V * (TAPS + 3) * width * width,
            bytes_accessed=10 * MIB,
            transcendentals=0,
        ),
        name="data_gradient",
    )(neighbours, core, grad_in, occ_rows, weight)


def finish_kernel(
    core_ref, grad_ref, r0, r1, ra, rb, feat_ref, occ_ref, buf_ref, after_ref, out_ref, work_ref
):
    width = feat_ref.shape[2]
    work_ref[...] = grad_ref[...]
    first = core_ref[0] == 0
    came = (r0[0], r1[0], jnp.where(first, rb[0], ra[0]), jnp.where(first, ra[0], rb[0]))
    for f, far in enumerate(came):
        add_face(work_ref, 0, f, far.astype(jnp.float32))
    values = feat_ref[0].astype(jnp.float32)
    r = norm_scale(values)
    u = values * r
    sig = sigmoid(u)
    d_u = mask_of(occ_ref[0], width) * work_ref[0] * (sig * (1.0 + u * (1.0 - sig)))
    pulled = r * (d_u - u * jnp.mean(u * d_u, axis=-1, keepdims=True))
    out_ref[0] = (buf_ref[0].astype(jnp.float32) + pulled).astype(jnp.bfloat16)


def finish_call(core, grad, remote, features, occ_rows, grad_in, after):
    listed, _, width = features.shape
    return pl.pallas_call(
        finish_kernel,
        grid=(listed,),
        in_specs=[smem(), by_brick((V, width))]
        + [by_brick((FACE, width))] * 4
        + [by_brick((V, width)), by_brick((1, V)), by_brick((V, width))]
        + glance([after]),
        out_specs=by_brick((V, width)),
        out_shape=jax.ShapeDtypeStruct((listed, V, width), jnp.bfloat16),
        scratch_shapes=[pltpu.VMEM((1, V, width), jnp.float32)],
        compiler_params=params(56),
        cost_estimate=pl.CostEstimate(
            flops=0, bytes_accessed=10 * listed * V * width, transcendentals=listed * V * width
        ),
        name="input_gradient",
    )(core, grad, *remote, features, occ_rows, grad_in, after)


def body(features, occupancy, routes, neighbours, weight, cotangent):
    listed, _, width = features.shape
    slots = cotangent.shape[0]
    rows, columns = lax.axis_size("gx"), lax.axis_size("gy")
    depth = rows // 2
    p = lax.axis_index("gx").astype(jnp.int32)
    z, c = p // 2, p % 2
    core = c.reshape(1)
    occ_rows = occupancy.reshape(listed, 1, V)
    neighbours = inner_neighbours(neighbours, listed)
    steps = jnp.arange(slots, dtype=jnp.int32)
    def way_of(core_id):
        return 1 - 2 * core_id

    source_core = (c + steps) % 2
    from_place = (z - way_of(source_core) * (steps // 2)) % depth * 2 + source_core
    route = routes[:, 0]
    out_place = way_of(c) * (route // 2 - z) % depth * 2 + (route + c) % 2

    hidden, *layers = hidden_call(core, features, occ_rows)
    remote = [
        from_behind(layers[1], 1),
        from_behind(layers[0], -1),
        *column_pair(layers[2], layers[3]),
    ]
    came = [
        lax.all_to_all(part, "gx", 0, 0, tiled=True)
        for part in (cotangent[:, : V // 2], cotangent[:, V // 2 :])
    ]
    placed = forward_call(
        neighbours, out_place, core, hidden, layers, remote, features, occ_rows,
        weight.reshape(9, 3 * width, width), slots,
    )
    scale = float(listed * rows * columns * V) ** (-0.5)
    mine, theirs, grad_in = weight_call(
        neighbours, routes, core, hidden, layers, remote, came, occ_rows, scale, jnp.bfloat16,
        placed[0],
    )
    near, far, back = hold_call(placed[1:], came)
    near, far, back = hop(near, 1), hop(far, 1), hop(back, -1)
    near, far, back, theirs = hold_call([near, far, back, theirs], [mine])
    far = hop(far, 1)

    grad, *sends = data_call(neighbours, core, grad_in, occ_rows, weight)

    chip_sum = chip_call(mine, to_other_core(theirs), [far, grad])
    mate = to_other_core(jnp.stack([block[1] for block in (placed[0], near, far, back)]))
    same_core = [
        [(2 * layer + core_id) * columns + q for q in range(columns) for layer in range(depth)]
        for core_id in range(2)
    ]

    def all_to_all(pieces):
        return lax.all_to_all(
            pieces, ("gx", "gy"), 0, 0, axis_index_groups=same_core, tiled=True
        )

    parts = all_to_all(chip_sum.reshape(columns * depth, -1, width // 2))
    arrived = [
        from_behind(sends[0], -1), from_behind(sends[1], 1), *column_pair(sends[2], sends[3])
    ]

    token = sum(block[0, :16, :128].astype(jnp.float32) for block in [*arrived, mate])
    pieces = total_call(parts, columns * depth, [token])
    own = all_to_all(pieces)
    owned_out = collect_call(from_place, placed[0], near, far, back, mate, pieces)
    input_grad = finish_call(core, grad, arrived, features, occ_rows, grad_in, pieces)
    own = hold_call([own], [owned_out, input_grad])[0].reshape(chip_sum.shape)
    weight_grad = join_call(core, own, to_other_core(own), [owned_out, input_grad])
    return (owned_out, input_grad, weight_grad)


def solution(mesh):
    return jax.shard_map(
        body,
        mesh=mesh,
        in_specs=(
            P(("gx", "gy"), None, None),
            P(("gx", "gy"), None),
            P(("gx", "gy"), None),
            P(("gx", "gy"), None),
            P(),
            P(("gx", "gy"), None, None),
        ),
        out_specs=(P(("gx", "gy"), None, None), P(("gx", "gy"), None, None), P()),
        check_vma=False,
    )
```

```python
import jax
import jax.numpy as jnp
from jax import lax
from jax.experimental import pallas as pl
from jax.experimental.pallas import tpu as pltpu
from jax.sharding import PartitionSpec as P

EDGE = 8
TAPS = 27
V = 512
FACE = 64
PLANE = 80
MIB = 1 << 20

norm_eps = 1e-06


def from_behind(block, distance):
    count = lax.axis_size("gx")
    return lax.ppermute(block, "gx", [(i, (i + distance) % count) for i in range(count)])


def column_pair(first, second):
    rows, columns = lax.axis_size("gx"), lax.axis_size("gy")

    def shifted(block, sign):
        ways = []
        for p in range(rows):
            step = sign if p % 2 == 0 else -sign
            ways += [(p * columns + q, p * columns + (q + step) % columns) for q in range(columns)]
        return lax.ppermute(block, ("gx", "gy"), ways)

    return shifted(first, 1), shifted(second, -1)


def inner_neighbours(neighbours, listed):
    p, q = lax.axis_index("gx"), lax.axis_index("gy")
    inside = jnp.stack(
        [p > 0, p < lax.axis_size("gx") - 1, q > 0, q < lax.axis_size("gy") - 1, True, True]
    )
    return jnp.where(inside[None, :] | (neighbours < listed), neighbours, 2 * listed)


def hop(blocks, sign):
    count = lax.axis_size("gx")
    ways = [
        (p, (p // 2 + (sign if p % 2 == 0 else -sign)) * 2 % count + p % 2)
        for p in range(count)
    ]
    return lax.ppermute(blocks, "gx", ways)


def to_other_core(block):
    return lax.ppermute(block, "gx", [(p, p ^ 1) for p in range(lax.axis_size("gx"))])


def params(limit):
    return pltpu.CompilerParams(vmem_limit_bytes=limit * MIB)


def whole(shape):
    zeros = (0,) * len(shape)
    return pl.BlockSpec(shape, lambda *_: zeros)


def by_brick(shape):
    zeros = (0,) * len(shape)
    return pl.BlockSpec((1,) + shape, lambda s, *_: (s,) + zeros)


def smem():
    return pl.BlockSpec(memory_space=pltpu.SMEM)


def anywhere():
    return pl.BlockSpec(memory_space=pl.ANY)


def glance(arrays):
    specs = []
    for array in arrays:
        zeros = (0,) * array.ndim
        block = (1,) * (array.ndim - 2) + (16, 128)
        specs.append(pl.BlockSpec(block, lambda *_, zeros=zeros: zeros))
    return specs


def mask_of(occ_row, width):
    spread = jnp.broadcast_to(occ_row.astype(jnp.float32), (128, V))
    column = jnp.transpose(spread)
    return jnp.concatenate([column] * (width // 128), axis=1)


def norm_scale(values):
    return lax.rsqrt(jnp.mean(values * values, axis=-1, keepdims=True) + norm_eps)


def sigmoid(u):
    return 1.0 / (1.0 + jnp.exp(-u))


def hidden_kernel(core_ref, feat_ref, occ_ref, hid_ref, x0_ref, x1_ref, ya_ref, yb_ref):
    width = feat_ref.shape[2]
    values = feat_ref[0].astype(jnp.float32)
    u = values * norm_scale(values)
    hidden = mask_of(occ_ref[0], width) * (u * sigmoid(u))
    hid_ref[0] = hidden.astype(jnp.bfloat16)
    cube = hidden.reshape(EDGE, EDGE, EDGE, width)
    x0_ref[0] = cube[0].reshape(FACE, width).astype(jnp.bfloat16)
    x1_ref[0] = cube[EDGE - 1].reshape(FACE, width).astype(jnp.bfloat16)
    first = core_ref[0] == 0
    low, high = cube[:, 0].reshape(FACE, width), cube[:, EDGE - 1].reshape(FACE, width)
    ya_ref[0] = jnp.where(first, high, low).astype(jnp.bfloat16)
    yb_ref[0] = jnp.where(first, low, high).astype(jnp.bfloat16)


def hidden_call(core, features, occ_rows):
    listed, _, width = features.shape
    layer = jax.ShapeDtypeStruct((listed, FACE, width), jnp.bfloat16)
    return pl.pallas_call(
        hidden_kernel,
        grid=(listed,),
        in_specs=[smem(), by_brick((V, width)), by_brick((1, V))],
        out_specs=[by_brick((V, width))] + [by_brick((FACE, width))] * 4,
        out_shape=[jax.ShapeDtypeStruct((listed, V, width), jnp.bfloat16)] + [layer] * 4,
        compiler_params=params(16),
        name="hidden",
    )(core, features, occ_rows)


def hold_kernel(*refs):
    pass


def hold_call(blocks, after):
    return pl.pallas_call(
        hold_kernel,
        grid=(1,),
        in_specs=[anywhere()] * len(blocks) + glance(after),
        out_specs=[anywhere()] * len(blocks),
        out_shape=[jax.ShapeDtypeStruct(block.shape, block.dtype) for block in blocks],
        input_output_aliases={i: i for i in range(len(blocks))},
        compiler_params=params(16),
        name="hold",
    )(*blocks, *after)


def collect_kernel(
    place_ref, own_ref, near_ref, far_ref, back_ref, mate_ref, after_ref, out_ref
):
    for step, came_ref in enumerate((own_ref, near_ref, far_ref, back_ref)):
        out_ref[place_ref[2 * step]] = came_ref[0]
        out_ref[place_ref[2 * step + 1]] = mate_ref[step]


def collect_call(place, own, near, far, back, mate, after):
    shape = (2 * mate.shape[0],) + mate.shape[1:]
    return pl.pallas_call(
        collect_kernel,
        grid=(1,),
        in_specs=[smem()] + [whole(own.shape)] * 4 + [whole(mate.shape)] + glance([after]),
        out_specs=whole(shape),
        out_shape=jax.ShapeDtypeStruct(shape, mate.dtype),
        compiler_params=params(20),
        cost_estimate=pl.CostEstimate(
            flops=0, bytes_accessed=4 * shape[0] * shape[1] * shape[2], transcendentals=0
        ),
        name="collect",
    )(place, own, near, far, back, mate, after)


def roll_c(block, shift):
    flat = block.reshape((-1,) + block.shape[-2:])
    return pltpu.roll(flat, shift % EDGE, 1).reshape(block.shape)


def c_index(shape):
    return lax.broadcasted_iota(jnp.int32, shape, len(shape) - 2)


def extended_brick(s, near_ref, core_ref, hid_ref, own, far, store):
    listed, _, width = hid_ref.shape

    def flag(condition):
        return jnp.where(condition, 1.0, 0.0).astype(jnp.float32)

    first = core_ref[0] == 0

    def face(f):
        n = near_ref[s, f]
        at_here, at_there = jnp.minimum(n, listed - 1), jnp.clip(n - listed, 0, listed - 1)
        if f < 2:
            here, there = own[f ^ 1][at_here], far[f][at_there]
        else:
            a, b = (2, 3) if f == 2 else (3, 2)
            here = jnp.where(first, own[a][at_here], own[b][at_here])
            there = jnp.where(first, far[a][at_there], far[b][at_there])
        here, there = here.astype(jnp.float32), there.astype(jnp.float32)
        value = here * flag(n < listed) + there * flag((n >= listed) & (n < 2 * listed))
        return value.reshape(EDGE, EDGE, width)

    def column(f):
        n = near_ref[s, f]
        brick = hid_ref[jnp.minimum(n, listed - 1)].astype(jnp.float32) * flag(n < listed)
        return brick.reshape(EDGE, EDGE, EDGE, width)

    def extended(core, sides):
        x0, x1, y0, y1 = sides
        blank = jnp.zeros((1, EDGE, width), jnp.float32)
        middle = jnp.concatenate([y0[:, None], core, y1[:, None]], axis=1)
        first = jnp.concatenate([blank, x0, blank], axis=0)[None]
        last = jnp.concatenate([blank, x1, blank], axis=0)[None]
        return jnp.concatenate([first, middle, last], axis=0)

    def put(k, block):
        everything = block.reshape(EDGE + 2, PLANE, width).astype(jnp.bfloat16)
        inner = block[:, 1 : EDGE + 1].reshape(EDGE + 2, FACE, width).astype(jnp.bfloat16)
        store(k, everything, inner)

    core = hid_ref[s].astype(jnp.float32).reshape(EDGE, EDGE, EDGE, width)
    sides = [face(f) for f in range(4)]
    at = c_index(core.shape)
    at_side = c_index(sides[0].shape)
    for k, edge, f in ((0, EDGE - 1, 4), (2, 0, 5)):
        shown = extended(
            jnp.where(at == edge, column(f), core),
            [jnp.where(at_side == edge, 0.0, side) for side in sides],
        )
        put(k, roll_c(shown, 1 - k))
    put(1, extended(core, sides))


def window(even_ref, odd_ref, s, i, j, k):
    if j == 1:
        part = odd_ref[s, k, pl.ds(i, EDGE)]
    else:
        part = even_ref[s, k, pl.ds(i, EDGE), j * EDGE : j * EDGE + FACE]
    return part.reshape(V, part.shape[-1])


def forward_kernel(
    near_ref, place_ref, core_ref, hid_ref, l0, l1, l2, l3, r0, r1, r2, r3, feat_ref, occ_ref, w_ref,
    *refs,
):
    outs, even_ref, odd_ref = refs[:-2], refs[-2], refs[-1]
    s = pl.program_id(0)
    width = feat_ref.shape[2]

    @pl.when(s == 0)
    def _():
        for out_ref in outs:
            out_ref[...] = jnp.zeros_like(out_ref)

    def store(k, everything, inner):
        even_ref[0, k] = everything
        odd_ref[0, k] = inner

    extended_brick(s, near_ref, core_ref, hid_ref, (l0, l1, l2, l3), (r0, r1, r2, r3), store)
    total = jnp.zeros((V, width), jnp.float32)
    for i in range(3):
        for j in range(3):
            rows = jnp.concatenate(
                [window(even_ref, odd_ref, 0, i, j, k) for k in range(3)], axis=1
            )
            total = total + jnp.dot(rows, w_ref[3 * i + j], preferred_element_type=jnp.float32)
    result = feat_ref[0].astype(jnp.float32) + mask_of(occ_ref[0], width) * total
    result = result.astype(jnp.bfloat16)
    for step, out_ref in enumerate(outs):

        @pl.when(place_ref[s] // 2 == step)
        def _():
            out_ref[place_ref[s] % 2] = result


def extended_scratch(bricks, width):
    return [
        pltpu.VMEM((bricks, 3, EDGE + 2, PLANE, width), jnp.bfloat16),
        pltpu.VMEM((bricks, 3, EDGE + 2, FACE, width), jnp.bfloat16),
    ]


def forward_call(
    neighbours, place, core, hidden, layers, remote, features, occ_rows, weight9, slots
):
    listed, _, width = features.shape
    layer = whole((listed, FACE, width))
    return pl.pallas_call(
        forward_kernel,
        grid=(listed,),
        in_specs=[smem(), smem(), smem(), whole((listed, V, width))]
        + [layer] * 8
        + [by_brick((V, width)), by_brick((1, V)), whole(weight9.shape)],
        out_specs=[whole((2, V, width))] * (slots // 2),
        out_shape=[jax.ShapeDtypeStruct((2, V, width), jnp.bfloat16)] * (slots // 2),
        scratch_shapes=extended_scratch(1, width),
        compiler_params=params(56),
        cost_estimate=pl.CostEstimate(
            flops=2 * listed * V * TAPS * width * width,
            bytes_accessed=10 * MIB,
            transcendentals=0,
        ),
        name="forward",
    )(neighbours, place, core, hidden, *layers, *remote, features, occ_rows, weight9)


def weight_kernel(
    near_ref, place_ref, core_ref, hid_ref, l0, l1, l2, l3, r0, r1, r2, r3, occ_ref, after_ref,
    *refs, scale,
):
    came, refs = refs[:-7], refs[-7:]
    mine_ref, theirs_ref, grad_ref, even_ref, odd_ref, turned_ref, sem = refs
    part = V // len(came)
    i = pl.program_id(0)
    listed, _, width = hid_ref.shape
    half = width // 2

    def copy(t, s):
        return pltpu.make_async_copy(
            came[t].at[place_ref[s, 0]],
            grad_ref.at[s, pl.ds(t * part, part)],
            sem.at[t * listed + s],
        )

    @pl.when(i == 0)
    def _():
        for s in range(listed):
            for t in range(len(came)):
                copy(t, s).start()

        @pl.loop(0, listed)
        def _(s):
            def store(k, everything, inner):
                even_ref[s, k] = everything
                odd_ref[s, k] = inner

            extended_brick(s, near_ref, core_ref, hid_ref, (l0, l1, l2, l3), (r0, r1, r2, r3), store)

        for s in range(listed):
            for t in range(len(came)):
                copy(t, s).wait()
            mixed = grad_ref[s].astype(jnp.float32) * mask_of(occ_ref[s], width)
            turned_ref[:, s * V : (s + 1) * V] = jnp.transpose(mixed).astype(jnp.bfloat16)

    @pl.when(i < 3)
    def _():
        first = core_ref[0] == 0
        for j in range(3):
            for k in range(3):
                rows = jnp.concatenate(
                    [window(even_ref, odd_ref, s, i, j, k) for s in range(listed)], axis=0
                )
                product = jnp.dot(turned_ref[...], rows, preferred_element_type=jnp.float32)
                product = jnp.transpose(product) * scale
                low, high = product[:, :half], product[:, half:]
                mine_ref[3 * j + k] = jnp.where(first, low, high)
                theirs_ref[3 * j + k] = jnp.where(first, high, low).astype(theirs_ref.dtype)

    @pl.when(i == 3)
    def _():
        mine_ref[...] = jnp.zeros_like(mine_ref)
        theirs_ref[...] = jnp.zeros_like(theirs_ref)


def weight_call(
    neighbours, place, core, hidden, layers, remote, came, occ_rows, scale, kind, after
):
    listed, _, width = hidden.shape
    shape = (TAPS + 1, width, width // 2)
    block = pl.BlockSpec((9, width, width // 2), lambda i: (i, 0, 0))
    return pl.pallas_call(
        lambda *refs: weight_kernel(*refs, scale=scale),
        grid=(4,),
        in_specs=[smem(), smem(), smem(), whole(hidden.shape)]
        + [whole((listed, FACE, width))] * 8
        + [whole(occ_rows.shape)]
        + glance([after])
        + [anywhere()] * len(came),
        out_specs=[block, block, whole(hidden.shape)],
        out_shape=[
            jax.ShapeDtypeStruct(shape, jnp.float32),
            jax.ShapeDtypeStruct(shape, kind),
            jax.ShapeDtypeStruct(hidden.shape, jnp.bfloat16),
        ],
        scratch_shapes=extended_scratch(listed, width)
        + [pltpu.VMEM((width, listed * V), jnp.bfloat16), pltpu.SemaphoreType.DMA((len(came) * listed,))],
        compiler_params=params(32),
        cost_estimate=pl.CostEstimate(
            flops=2 * listed * V * TAPS * width * width,
            bytes_accessed=10 * MIB,
            transcendentals=0,
        ),
        name="weight_gradient",
    )(neighbours, place, core, hidden, *layers, *remote, occ_rows, after, *came)


def chip_kernel(mine_ref, theirs_ref, *refs):
    out_ref = refs[-1]
    added = mine_ref[...] + theirs_ref[...].astype(jnp.float32)
    out_ref[...] = added.astype(jnp.bfloat16)


def chip_call(mine, theirs, after):
    taps, width, half = mine.shape
    block = pl.BlockSpec((7, width, half), lambda t: (t, 0, 0))
    return pl.pallas_call(
        chip_kernel,
        grid=(taps // 7,),
        in_specs=[block, block] + glance(after),
        out_specs=block,
        out_shape=jax.ShapeDtypeStruct(mine.shape, jnp.bfloat16),
        compiler_params=params(12),
        name="chip_sum",
    )(mine, theirs, *after)


def total_kernel(parts_ref, *refs):
    out_ref = refs[-1]
    total = jnp.sum(parts_ref[...].astype(jnp.float32), axis=0)
    for z in range(out_ref.shape[0]):
        out_ref[z] = total.astype(jnp.bfloat16)


def total_call(parts, copies, after):
    _, rows, half = parts.shape
    return pl.pallas_call(
        total_kernel,
        grid=(1,),
        in_specs=[whole(parts.shape)] + glance(after),
        out_specs=whole((copies, rows, half)),
        out_shape=jax.ShapeDtypeStruct((copies, rows, half), jnp.bfloat16),
        compiler_params=params(20),
        name="total",
    )(parts, *after)


def half_kernel(core_ref, block_ref, *refs):
    refs[-1][...] = block_ref[...].astype(jnp.float32)


def half_call(core, block, is_other, base):
    _, width, half = block.shape

    def place(t, core_ref):
        return t, 0, (1 - core_ref[0] if is_other else core_ref[0])

    return pl.pallas_call(
        half_kernel,
        grid_spec=pltpu.PrefetchScalarGridSpec(
            num_scalar_prefetch=1,
            grid=(TAPS // 9,),
            in_specs=[pl.BlockSpec((9, width, half), lambda t, core_ref: (t, 0, 0))]
            + [anywhere()] * len(base),
            out_specs=pl.BlockSpec((9, width, half), place),
        ),
        out_shape=jax.ShapeDtypeStruct((TAPS, width, 2 * half), jnp.float32),
        input_output_aliases={2: 0} if base else {},
        compiler_params=params(16),
        cost_estimate=pl.CostEstimate(
            flops=0, bytes_accessed=6 * TAPS * width * half, transcendentals=0
        ),
        name="half",
    )(core, block, *base)


def data_kernel(
    near_ref, core_ref, buf_ref, occ_ref, w_ref,
    grad_ref, s0_ref, s1_ref, sa_ref, sb_ref,
    wide_ref, rows_ref, depth_ref, kept_ref,
):
    s = pl.program_id(0)
    listed = grad_ref.shape[0]
    width = buf_ref.shape[2]
    last = s == listed - 1

    mixed = buf_ref[0].astype(jnp.float32) * mask_of(occ_ref[0], width)
    cube = mixed.reshape(FACE, EDGE, width)
    at = c_index(cube.shape)

    def three(block, index):
        ahead = jnp.where(index == EDGE - 1, 0.0, roll_c(block, -1))
        behind = jnp.where(index == 0, 0.0, roll_c(block, 1))
        flat = (-1, width)
        return [entry.reshape(flat).astype(jnp.bfloat16) for entry in (ahead, block, behind)]

    def back(rows, taps):
        return sum(
            lax.dot_general(
                row, w_ref[tap], (((1,), (1,)), ((), ())), preferred_element_type=jnp.float32
            )
            for row, tap in zip(rows, taps)
        )

    rows = three(cube, at)
    wide_ref[...] = jnp.zeros_like(wide_ref)
    for i in range(3):
        for j in range(3):
            product = back(rows, [9 * i + 3 * j + k for k in range(3)])
            wide_ref[i : i + EDGE, j * EDGE : j * EDGE + FACE] += product.reshape(
                EDGE, FACE, width
            )

    def rounded(block):
        return block.astype(jnp.bfloat16).astype(jnp.float32)

    inside = slice(EDGE, EDGE + FACE)
    grad_ref[s] = rounded(wide_ref[1 : EDGE + 1, inside].reshape(V, width))
    kept_ref[s, 0] = rounded(wide_ref[0, inside])
    kept_ref[s, 1] = rounded(wide_ref[EDGE + 1, inside])
    kept_ref[s, 2] = rounded(wide_ref[1 : EDGE + 1, 0:EDGE].reshape(FACE, width))
    kept_ref[s, 3] = rounded(wide_ref[1 : EDGE + 1, PLANE - EDGE : PLANE].reshape(FACE, width))

    halves = range(width // 128)
    for half in halves:
        rows_ref[half] = mixed[:, half * 128 : (half + 1) * 128]
    for side, c in ((0, 0), (1, EDGE - 1)):
        layer = jnp.concatenate(
            [rows_ref[half, pl.ds(c, FACE, stride=EDGE)] for half in halves], axis=1
        )
        layer = layer.reshape(EDGE, EDGE, width)
        for j, entry in enumerate(three(layer, c_index(layer.shape))):
            depth_ref[side, j, pl.ds(s * FACE, FACE)] = entry

    @pl.when(last)
    def _():
        for side in range(2):
            total = jnp.zeros((listed, EDGE + 2, EDGE, width), jnp.float32)
            for i in range(3):
                product = back(
                    [depth_ref[side, j] for j in range(3)],
                    [9 * i + 3 * j + 2 * side for j in range(3)],
                ).reshape(listed, EDGE, EDGE, width)
                pieces = [product]
                if i > 0:
                    pieces.insert(0, jnp.zeros((listed, i, EDGE, width), jnp.float32))
                if i < 2:
                    pieces.append(jnp.zeros((listed, 2 - i, EDGE, width), jnp.float32))
                total = total + jnp.concatenate(pieces, axis=1)
            rows_ref[...] = jnp.zeros_like(rows_ref)
            for h in range(listed):
                n = near_ref[h, 4 + side]

                @pl.when(n < listed)
                def _():
                    piece = rounded(total[h, 1 : EDGE + 1].reshape(FACE, width))
                    c = (EDGE - 1) * (1 - side)
                    for half in halves:
                        rows_ref[half, pl.ds(c, FACE, stride=EDGE)] = piece[
                            :, half * 128 : (half + 1) * 128
                        ]
                    grad_ref[n] += jnp.concatenate([rows_ref[half] for half in halves], axis=1)

        leaving = []
        for f in range(4):
            sums = [jnp.zeros((FACE, width), jnp.float32) for _ in range(listed)]
            for h in range(listed):
                n = near_ref[h, f]
                piece = kept_ref[h, f]
                sums = [
                    total + piece * jnp.where(n == listed + t, 1.0, 0.0).astype(jnp.float32)
                    for t, total in enumerate(sums)
                ]

                @pl.when(n < listed)
                def _():
                    add_face(grad_ref, n, f, piece)

            leaving.append(sums)
        first = core_ref[0] == 0
        for t in range(listed):
            s0_ref[t] = leaving[0][t].astype(jnp.bfloat16)
            s1_ref[t] = leaving[1][t].astype(jnp.bfloat16)
            sa_ref[t] = jnp.where(first, leaving[3][t], leaving[2][t]).astype(jnp.bfloat16)
            sb_ref[t] = jnp.where(first, leaving[2][t], leaving[3][t]).astype(jnp.bfloat16)


def add_face(ref, n, f, piece):
    near_end = f % 2 == 1
    if f < 2:
        start = 0 if near_end else V - FACE
        ref[n, start : start + FACE] += piece
    else:
        for a in range(EDGE):
            start = a * FACE + (0 if near_end else FACE - EDGE)
            ref[n, start : start + EDGE] += piece[a * EDGE : (a + 1) * EDGE]


def data_call(neighbours, core, grad_in, occ_rows, weight):
    listed, _, width = grad_in.shape
    layer = jax.ShapeDtypeStruct((listed, FACE, width), jnp.bfloat16)
    return pl.pallas_call(
        data_kernel,
        grid=(listed,),
        in_specs=[smem(), smem(), by_brick((V, width)), by_brick((1, V)), whole(weight.shape)],
        out_specs=[whole((listed, V, width))] + [whole(layer.shape)] * 4,
        out_shape=[jax.ShapeDtypeStruct((listed, V, width), jnp.float32)] + [layer] * 4,
        scratch_shapes=[
            pltpu.VMEM((EDGE + 2, PLANE, width), jnp.float32),
            pltpu.VMEM((width // 128, V, 128), jnp.float32),
            pltpu.VMEM((2, 3, listed * FACE, width), jnp.bfloat16),
            pltpu.VMEM((listed, 4, FACE, width), jnp.float32),
        ],
        compiler_params=params(32),
        cost_estimate=pl.CostEstimate(
            flops=2 * listed * V * (TAPS + 3) * width * width,
            bytes_accessed=10 * MIB,
            transcendentals=0,
        ),
        name="data_gradient",
    )(neighbours, core, grad_in, occ_rows, weight)


def finish_kernel(
    core_ref, grad_ref, r0, r1, ra, rb, feat_ref, occ_ref, buf_ref, after_ref, out_ref, work_ref
):
    width = feat_ref.shape[2]
    work_ref[...] = grad_ref[...]
    first = core_ref[0] == 0
    came = (r0[0], r1[0], jnp.where(first, rb[0], ra[0]), jnp.where(first, ra[0], rb[0]))
    for f, far in enumerate(came):
        add_face(work_ref, 0, f, far.astype(jnp.float32))
    values = feat_ref[0].astype(jnp.float32)
    r = norm_scale(values)
    u = values * r
    sig = sigmoid(u)
    d_u = mask_of(occ_ref[0], width) * work_ref[0] * (sig * (1.0 + u * (1.0 - sig)))
    pulled = r * (d_u - u * jnp.mean(u * d_u, axis=-1, keepdims=True))
    out_ref[0] = (buf_ref[0].astype(jnp.float32) + pulled).astype(jnp.bfloat16)


def finish_call(core, grad, remote, features, occ_rows, grad_in, after):
    listed, _, width = features.shape
    return pl.pallas_call(
        finish_kernel,
        grid=(listed,),
        in_specs=[smem(), by_brick((V, width))]
        + [by_brick((FACE, width))] * 4
        + [by_brick((V, width)), by_brick((1, V)), by_brick((V, width))]
        + glance([after]),
        out_specs=by_brick((V, width)),
        out_shape=jax.ShapeDtypeStruct((listed, V, width), jnp.bfloat16),
        scratch_shapes=[pltpu.VMEM((1, V, width), jnp.float32)],
        compiler_params=params(56),
        cost_estimate=pl.CostEstimate(
            flops=0, bytes_accessed=10 * listed * V * width, transcendentals=listed * V * width
        ),
        name="input_gradient",
    )(core, grad, *remote, features, occ_rows, grad_in, after)


def body(features, occupancy, routes, neighbours, weight, cotangent):
    listed, _, width = features.shape
    slots = cotangent.shape[0]
    rows, columns = lax.axis_size("gx"), lax.axis_size("gy")
    depth = rows // 2
    p = lax.axis_index("gx").astype(jnp.int32)
    z, c = p // 2, p % 2
    core = c.reshape(1)
    occ_rows = occupancy.reshape(listed, 1, V)
    neighbours = inner_neighbours(neighbours, listed)
    steps = jnp.arange(slots, dtype=jnp.int32)
    def way_of(core_id):
        return 1 - 2 * core_id

    source_core = (c + steps) % 2
    from_place = (z - way_of(source_core) * (steps // 2)) % depth * 2 + source_core
    route = routes[:, 0]
    out_place = way_of(c) * (route // 2 - z) % depth * 2 + (route + c) % 2

    hidden, *layers = hidden_call(core, features, occ_rows)
    remote = [
        from_behind(layers[1], 1),
        from_behind(layers[0], -1),
        *column_pair(layers[2], layers[3]),
    ]
    came = [
        lax.all_to_all(part, "gx", 0, 0, tiled=True)
        for part in (cotangent[:, : V // 2], cotangent[:, V // 2 :])
    ]
    placed = forward_call(
        neighbours, out_place, core, hidden, layers, remote, features, occ_rows,
        weight.reshape(9, 3 * width, width), slots,
    )
    scale = float(listed * rows * columns * V) ** (-0.5)
    mine, theirs, grad_in = weight_call(
        neighbours, routes, core, hidden, layers, remote, came, occ_rows, scale, jnp.bfloat16,
        placed[0],
    )
    near, far, back = hold_call(placed[1:], came)
    near, far, back = hop(near, 1), hop(far, 1), hop(back, -1)
    near, far, back, theirs = hold_call([near, far, back, theirs], [mine])
    far = hop(far, 1)

    grad, *sends = data_call(neighbours, core, grad_in, occ_rows, weight)

    chip_sum = chip_call(mine, to_other_core(theirs), [far, grad])
    mate = to_other_core(jnp.stack([block[1] for block in (placed[0], near, far, back)]))
    same_core = [
        [(2 * layer + core_id) * columns + q for q in range(columns) for layer in range(depth)]
        for core_id in range(2)
    ]

    def all_to_all(pieces):
        return lax.all_to_all(
            pieces, ("gx", "gy"), 0, 0, axis_index_groups=same_core, tiled=True
        )

    parts = all_to_all(chip_sum.reshape(columns * depth, -1, width // 2))
    arrived = [
        from_behind(sends[0], -1), from_behind(sends[1], 1), *column_pair(sends[2], sends[3])
    ]

    token = sum(block[0, :16, :128].astype(jnp.float32) for block in [*arrived, mate])
    pieces = total_call(parts, columns * depth, [token])
    own = all_to_all(pieces)
    owned_out = collect_call(from_place, placed[0], near, far, back, mate, pieces)
    input_grad = finish_call(core, grad, arrived, features, occ_rows, grad_in, pieces)
    token = sum(block[0, :16, :128].astype(jnp.float32) for block in (owned_out, input_grad))
    own = hold_call([own], [token])[0].reshape(chip_sum.shape)
    weight_grad = half_call(core, own, False, [])
    weight_grad = half_call(core, to_other_core(own), True, [weight_grad])
    return (owned_out, input_grad, weight_grad)


def solution(mesh):
    return jax.shard_map(
        body,
        mesh=mesh,
        in_specs=(
            P(("gx", "gy"), None, None),
            P(("gx", "gy"), None),
            P(("gx", "gy"), None),
            P(("gx", "gy"), None),
            P(),
            P(("gx", "gy"), None, None),
        ),
        out_specs=(P(("gx", "gy"), None, None), P(("gx", "gy"), None, None), P()),
        check_vma=False,
    )
```

```python
import jax
import jax.numpy as jnp
from jax import lax
from jax.experimental import pallas as pl
from jax.experimental.pallas import tpu as pltpu
from jax.sharding import PartitionSpec as P

EDGE = 8
TAPS = 27
V = 512
FACE = 64
PLANE = 80
MIB = 1 << 20

norm_eps = 1e-06


def from_behind(block, distance):
    count = lax.axis_size("gx")
    return lax.ppermute(block, "gx", [(i, (i + distance) % count) for i in range(count)])


def column_pair(first, second):
    rows, columns = lax.axis_size("gx"), lax.axis_size("gy")

    def shifted(block, sign):
        ways = []
        for p in range(rows):
            step = sign if p % 2 == 0 else -sign
            ways += [(p * columns + q, p * columns + (q + step) % columns) for q in range(columns)]
        return lax.ppermute(block, ("gx", "gy"), ways)

    return shifted(first, 1), shifted(second, -1)


def inner_neighbours(neighbours, listed):
    p, q = lax.axis_index("gx"), lax.axis_index("gy")
    inside = jnp.stack(
        [p > 0, p < lax.axis_size("gx") - 1, q > 0, q < lax.axis_size("gy") - 1, True, True]
    )
    return jnp.where(inside[None, :] | (neighbours < listed), neighbours, 2 * listed)


def hop(blocks, sign):
    count = lax.axis_size("gx")
    ways = [
        (p, (p // 2 + (sign if p % 2 == 0 else -sign)) * 2 % count + p % 2)
        for p in range(count)
    ]
    return lax.ppermute(blocks, "gx", ways)


def to_other_core(block):
    return lax.ppermute(block, "gx", [(p, p ^ 1) for p in range(lax.axis_size("gx"))])


def params(limit):
    return pltpu.CompilerParams(vmem_limit_bytes=limit * MIB)


def whole(shape):
    zeros = (0,) * len(shape)
    return pl.BlockSpec(shape, lambda *_: zeros)


def by_brick(shape):
    zeros = (0,) * len(shape)
    return pl.BlockSpec((1,) + shape, lambda s, *_: (s,) + zeros)


def smem():
    return pl.BlockSpec(memory_space=pltpu.SMEM)


def anywhere():
    return pl.BlockSpec(memory_space=pl.ANY)


def glance(arrays):
    specs = []
    for array in arrays:
        zeros = (0,) * array.ndim
        block = (1,) * (array.ndim - 2) + (16, 128)
        specs.append(pl.BlockSpec(block, lambda *_, zeros=zeros: zeros))
    return specs


def mask_of(occ_row, width):
    spread = jnp.broadcast_to(occ_row.astype(jnp.float32), (128, V))
    column = jnp.transpose(spread)
    return jnp.concatenate([column] * (width // 128), axis=1)


def norm_scale(values):
    return lax.rsqrt(jnp.mean(values * values, axis=-1, keepdims=True) + norm_eps)


def sigmoid(u):
    return 1.0 / (1.0 + jnp.exp(-u))


def hidden_kernel(core_ref, feat_ref, occ_ref, hid_ref, x0_ref, x1_ref, ya_ref, yb_ref):
    width = feat_ref.shape[2]
    values = feat_ref[0].astype(jnp.float32)
    u = values * norm_scale(values)
    hidden = mask_of(occ_ref[0], width) * (u * sigmoid(u))
    hid_ref[0] = hidden.astype(jnp.bfloat16)
    cube = hidden.reshape(EDGE, EDGE, EDGE, width)
    x0_ref[0] = cube[0].reshape(FACE, width).astype(jnp.bfloat16)
    x1_ref[0] = cube[EDGE - 1].reshape(FACE, width).astype(jnp.bfloat16)
    first = core_ref[0] == 0
    low, high = cube[:, 0].reshape(FACE, width), cube[:, EDGE - 1].reshape(FACE, width)
    ya_ref[0] = jnp.where(first, high, low).astype(jnp.bfloat16)
    yb_ref[0] = jnp.where(first, low, high).astype(jnp.bfloat16)


def hidden_call(core, features, occ_rows):
    listed, _, width = features.shape
    layer = jax.ShapeDtypeStruct((listed, FACE, width), jnp.bfloat16)
    return pl.pallas_call(
        hidden_kernel,
        grid=(listed,),
        in_specs=[smem(), by_brick((V, width)), by_brick((1, V))],
        out_specs=[by_brick((V, width))] + [by_brick((FACE, width))] * 4,
        out_shape=[jax.ShapeDtypeStruct((listed, V, width), jnp.bfloat16)] + [layer] * 4,
        compiler_params=params(16),
        name="hidden",
    )(core, features, occ_rows)


def hold_kernel(*refs):
    pass


def hold_call(blocks, after):
    return pl.pallas_call(
        hold_kernel,
        grid=(1,),
        in_specs=[anywhere()] * len(blocks) + glance(after),
        out_specs=[anywhere()] * len(blocks),
        out_shape=[jax.ShapeDtypeStruct(block.shape, block.dtype) for block in blocks],
        input_output_aliases={i: i for i in range(len(blocks))},
        compiler_params=params(16),
        name="hold",
    )(*blocks, *after)


def collect_kernel(
    place_ref, own_ref, near_ref, far_ref, back_ref, mate_ref, after_ref, out_ref
):
    for step, came_ref in enumerate((own_ref, near_ref, far_ref, back_ref)):
        out_ref[place_ref[2 * step]] = came_ref[0]
        out_ref[place_ref[2 * step + 1]] = mate_ref[step]


def collect_call(place, own, near, far, back, mate, after):
    shape = (2 * mate.shape[0],) + mate.shape[1:]
    return pl.pallas_call(
        collect_kernel,
        grid=(1,),
        in_specs=[smem()] + [whole(own.shape)] * 4 + [whole(mate.shape)] + glance([after]),
        out_specs=whole(shape),
        out_shape=jax.ShapeDtypeStruct(shape, mate.dtype),
        compiler_params=params(20),
        cost_estimate=pl.CostEstimate(
            flops=0, bytes_accessed=4 * shape[0] * shape[1] * shape[2], transcendentals=0
        ),
        name="collect",
    )(place, own, near, far, back, mate, after)


def roll_c(block, shift):
    flat = block.reshape((-1,) + block.shape[-2:])
    return pltpu.roll(flat, shift % EDGE, 1).reshape(block.shape)


def c_index(shape):
    return lax.broadcasted_iota(jnp.int32, shape, len(shape) - 2)


def extended_brick(s, near_ref, core_ref, hid_ref, own, far, store):
    listed, _, width = hid_ref.shape

    def flag(condition):
        return jnp.where(condition, 1.0, 0.0).astype(jnp.float32)

    first = core_ref[0] == 0

    def face(f):
        n = near_ref[s, f]
        at_here, at_there = jnp.minimum(n, listed - 1), jnp.clip(n - listed, 0, listed - 1)
        if f < 2:
            here, there = own[f ^ 1][at_here], far[f][at_there]
        else:
            a, b = (2, 3) if f == 2 else (3, 2)
            here = jnp.where(first, own[a][at_here], own[b][at_here])
            there = jnp.where(first, far[a][at_there], far[b][at_there])
        here, there = here.astype(jnp.float32), there.astype(jnp.float32)
        value = here * flag(n < listed) + there * flag((n >= listed) & (n < 2 * listed))
        return value.reshape(EDGE, EDGE, width)

    def column(f):
        n = near_ref[s, f]
        brick = hid_ref[jnp.minimum(n, listed - 1)].astype(jnp.float32) * flag(n < listed)
        return brick.reshape(EDGE, EDGE, EDGE, width)

    def extended(core, sides):
        x0, x1, y0, y1 = sides
        blank = jnp.zeros((1, EDGE, width), jnp.float32)
        middle = jnp.concatenate([y0[:, None], core, y1[:, None]], axis=1)
        first = jnp.concatenate([blank, x0, blank], axis=0)[None]
        last = jnp.concatenate([blank, x1, blank], axis=0)[None]
        return jnp.concatenate([first, middle, last], axis=0)

    def put(k, block):
        everything = block.reshape(EDGE + 2, PLANE, width).astype(jnp.bfloat16)
        inner = block[:, 1 : EDGE + 1].reshape(EDGE + 2, FACE, width).astype(jnp.bfloat16)
        store(k, everything, inner)

    core = hid_ref[s].astype(jnp.float32).reshape(EDGE, EDGE, EDGE, width)
    sides = [face(f) for f in range(4)]
    at = c_index(core.shape)
    at_side = c_index(sides[0].shape)
    for k, edge, f in ((0, EDGE - 1, 4), (2, 0, 5)):
        shown = extended(
            jnp.where(at == edge, column(f), core),
            [jnp.where(at_side == edge, 0.0, side) for side in sides],
        )
        put(k, roll_c(shown, 1 - k))
    put(1, extended(core, sides))


def window(even_ref, odd_ref, s, i, j, k):
    if j == 1:
        part = odd_ref[s, k, pl.ds(i, EDGE)]
    else:
        part = even_ref[s, k, pl.ds(i, EDGE), j * EDGE : j * EDGE + FACE]
    return part.reshape(V, part.shape[-1])


def forward_kernel(
    near_ref, place_ref, core_ref, hid_ref, l0, l1, l2, l3, r0, r1, r2, r3, feat_ref, occ_ref, w_ref,
    *refs,
):
    outs, even_ref, odd_ref = refs[:-2], refs[-2], refs[-1]
    s = pl.program_id(0)
    width = feat_ref.shape[2]

    @pl.when(s == 0)
    def _():
        for out_ref in outs:
            out_ref[...] = jnp.zeros_like(out_ref)

    def store(k, everything, inner):
        even_ref[0, k] = everything
        odd_ref[0, k] = inner

    extended_brick(s, near_ref, core_ref, hid_ref, (l0, l1, l2, l3), (r0, r1, r2, r3), store)
    total = jnp.zeros((V, width), jnp.float32)
    for i in range(3):
        for j in range(3):
            rows = jnp.concatenate(
                [window(even_ref, odd_ref, 0, i, j, k) for k in range(3)], axis=1
            )
            total = total + jnp.dot(rows, w_ref[3 * i + j], preferred_element_type=jnp.float32)
    result = feat_ref[0].astype(jnp.float32) + mask_of(occ_ref[0], width) * total
    result = result.astype(jnp.bfloat16)
    for step, out_ref in enumerate(outs):

        @pl.when(place_ref[s] // 2 == step)
        def _():
            out_ref[place_ref[s] % 2] = result


def extended_scratch(bricks, width):
    return [
        pltpu.VMEM((bricks, 3, EDGE + 2, PLANE, width), jnp.bfloat16),
        pltpu.VMEM((bricks, 3, EDGE + 2, FACE, width), jnp.bfloat16),
    ]


def forward_call(
    neighbours, place, core, hidden, layers, remote, features, occ_rows, weight9, slots
):
    listed, _, width = features.shape
    layer = whole((listed, FACE, width))
    return pl.pallas_call(
        forward_kernel,
        grid=(listed,),
        in_specs=[smem(), smem(), smem(), whole((listed, V, width))]
        + [layer] * 8
        + [by_brick((V, width)), by_brick((1, V)), whole(weight9.shape)],
        out_specs=[whole((2, V, width))] * (slots // 2),
        out_shape=[jax.ShapeDtypeStruct((2, V, width), jnp.bfloat16)] * (slots // 2),
        scratch_shapes=extended_scratch(1, width),
        compiler_params=params(56),
        cost_estimate=pl.CostEstimate(
            flops=2 * listed * V * TAPS * width * width,
            bytes_accessed=10 * MIB,
            transcendentals=0,
        ),
        name="forward",
    )(neighbours, place, core, hidden, *layers, *remote, features, occ_rows, weight9)


def weight_kernel(
    near_ref, place_ref, core_ref, hid_ref, l0, l1, l2, l3, r0, r1, r2, r3, occ_ref, after_ref,
    *refs, scale,
):
    came, refs = refs[:-7], refs[-7:]
    mine_ref, theirs_ref, grad_ref, even_ref, odd_ref, turned_ref, sem = refs
    part = V // len(came)
    i = pl.program_id(0)
    listed, _, width = hid_ref.shape
    half = width // 2

    def copy(t, s):
        return pltpu.make_async_copy(
            came[t].at[place_ref[s, 0]],
            grad_ref.at[s, pl.ds(t * part, part)],
            sem.at[t * listed + s],
        )

    @pl.when(i == 0)
    def _():
        for s in range(listed):
            for t in range(len(came)):
                copy(t, s).start()

        @pl.loop(0, listed)
        def _(s):
            def store(k, everything, inner):
                even_ref[s, k] = everything
                odd_ref[s, k] = inner

            extended_brick(s, near_ref, core_ref, hid_ref, (l0, l1, l2, l3), (r0, r1, r2, r3), store)

        for s in range(listed):
            for t in range(len(came)):
                copy(t, s).wait()
            mixed = grad_ref[s].astype(jnp.float32) * mask_of(occ_ref[s], width)
            turned_ref[:, s * V : (s + 1) * V] = jnp.transpose(mixed).astype(jnp.bfloat16)

    @pl.when(i < 3)
    def _():
        first = core_ref[0] == 0
        for j in range(3):
            for k in range(3):
                rows = jnp.concatenate(
                    [window(even_ref, odd_ref, s, i, j, k) for s in range(listed)], axis=0
                )
                product = jnp.dot(turned_ref[...], rows, preferred_element_type=jnp.float32)
                product = jnp.transpose(product) * scale
                low, high = product[:, :half], product[:, half:]
                mine_ref[3 * j + k] = jnp.where(first, low, high)
                theirs_ref[3 * j + k] = jnp.where(first, high, low).astype(theirs_ref.dtype)

    @pl.when(i == 3)
    def _():
        mine_ref[...] = jnp.zeros_like(mine_ref)
        theirs_ref[...] = jnp.zeros_like(theirs_ref)


def weight_call(
    neighbours, place, core, hidden, layers, remote, came, occ_rows, scale, kind, after
):
    listed, _, width = hidden.shape
    shape = (TAPS + 1, width, width // 2)
    block = pl.BlockSpec((9, width, width // 2), lambda i: (i, 0, 0))
    return pl.pallas_call(
        lambda *refs: weight_kernel(*refs, scale=scale),
        grid=(4,),
        in_specs=[smem(), smem(), smem(), whole(hidden.shape)]
        + [whole((listed, FACE, width))] * 8
        + [whole(occ_rows.shape)]
        + glance([after])
        + [anywhere()] * len(came),
        out_specs=[block, block, whole(hidden.shape)],
        out_shape=[
            jax.ShapeDtypeStruct(shape, jnp.float32),
            jax.ShapeDtypeStruct(shape, kind),
            jax.ShapeDtypeStruct(hidden.shape, jnp.bfloat16),
        ],
        scratch_shapes=extended_scratch(listed, width)
        + [pltpu.VMEM((width, listed * V), jnp.bfloat16), pltpu.SemaphoreType.DMA((len(came) * listed,))],
        compiler_params=params(32),
        cost_estimate=pl.CostEstimate(
            flops=2 * listed * V * TAPS * width * width,
            bytes_accessed=10 * MIB,
            transcendentals=0,
        ),
        name="weight_gradient",
    )(neighbours, place, core, hidden, *layers, *remote, occ_rows, after, *came)


def chip_kernel(mine_ref, theirs_ref, *refs):
    out_ref = refs[-1]
    added = mine_ref[...] + theirs_ref[...].astype(jnp.float32)
    out_ref[...] = added.astype(jnp.bfloat16)


def chip_call(mine, theirs, after):
    taps, width, half = mine.shape
    block = pl.BlockSpec((7, width, half), lambda t: (t, 0, 0))
    return pl.pallas_call(
        chip_kernel,
        grid=(taps // 7,),
        in_specs=[block, block] + glance(after),
        out_specs=block,
        out_shape=jax.ShapeDtypeStruct(mine.shape, jnp.bfloat16),
        compiler_params=params(12),
        name="chip_sum",
    )(mine, theirs, *after)


def total_kernel(parts_ref, *refs):
    out_ref = refs[-1]
    total = jnp.sum(parts_ref[...].astype(jnp.float32), axis=0)
    for z in range(out_ref.shape[0]):
        out_ref[z] = total.astype(jnp.bfloat16)


def total_call(parts, copies, after):
    _, rows, half = parts.shape
    return pl.pallas_call(
        total_kernel,
        grid=(1,),
        in_specs=[whole(parts.shape)] + glance(after),
        out_specs=whole((copies, rows, half)),
        out_shape=jax.ShapeDtypeStruct((copies, rows, half), jnp.bfloat16),
        compiler_params=params(20),
        name="total",
    )(parts, *after)


def half_kernel(core_ref, block_ref, *refs):
    refs[-1][...] = block_ref[...].astype(jnp.float32)


def half_call(core, block, is_other, base):
    _, width, half = block.shape

    def place(t, core_ref):
        return t, 0, (1 - core_ref[0] if is_other else core_ref[0])

    return pl.pallas_call(
        half_kernel,
        grid_spec=pltpu.PrefetchScalarGridSpec(
            num_scalar_prefetch=1,
            grid=(TAPS // 9,),
            in_specs=[pl.BlockSpec((9, width, half), lambda t, core_ref: (t, 0, 0))]
            + [anywhere()] * len(base),
            out_specs=pl.BlockSpec((9, width, half), place),
        ),
        out_shape=jax.ShapeDtypeStruct((TAPS, width, 2 * half), jnp.float32),
        input_output_aliases={2: 0} if base else {},
        compiler_params=params(16),
        cost_estimate=pl.CostEstimate(
            flops=0, bytes_accessed=6 * TAPS * width * half, transcendentals=0
        ),
        name="half",
    )(core, block, *base)


def data_kernel(
    near_ref, core_ref, buf_ref, occ_ref, w_ref,
    grad_ref, s0_ref, s1_ref, sa_ref, sb_ref,
    wide_ref, rows_ref, depth_ref, kept_ref,
):
    s = pl.program_id(0)
    listed = grad_ref.shape[0]
    width = buf_ref.shape[2]
    last = s == listed - 1

    mixed = buf_ref[0].astype(jnp.float32) * mask_of(occ_ref[0], width)
    cube = mixed.reshape(FACE, EDGE, width)
    at = c_index(cube.shape)

    def three(block, index):
        ahead = jnp.where(index == EDGE - 1, 0.0, roll_c(block, -1))
        behind = jnp.where(index == 0, 0.0, roll_c(block, 1))
        flat = (-1, width)
        return [entry.reshape(flat).astype(jnp.bfloat16) for entry in (ahead, block, behind)]

    def back(rows, taps):
        return sum(
            lax.dot_general(
                row, w_ref[tap], (((1,), (1,)), ((), ())), preferred_element_type=jnp.float32
            )
            for row, tap in zip(rows, taps)
        )

    rows = three(cube, at)
    wide_ref[...] = jnp.zeros_like(wide_ref)
    for i in range(3):
        for j in range(3):
            product = back(rows, [9 * i + 3 * j + k for k in range(3)])
            wide_ref[i : i + EDGE, j * EDGE : j * EDGE + FACE] += product.reshape(
                EDGE, FACE, width
            )

    def rounded(block):
        return block.astype(jnp.bfloat16).astype(jnp.float32)

    inside = slice(EDGE, EDGE + FACE)
    grad_ref[s] = rounded(wide_ref[1 : EDGE + 1, inside].reshape(V, width))
    kept_ref[s, 0] = rounded(wide_ref[0, inside])
    kept_ref[s, 1] = rounded(wide_ref[EDGE + 1, inside])
    kept_ref[s, 2] = rounded(wide_ref[1 : EDGE + 1, 0:EDGE].reshape(FACE, width))
    kept_ref[s, 3] = rounded(wide_ref[1 : EDGE + 1, PLANE - EDGE : PLANE].reshape(FACE, width))

    halves = range(width // 128)
    for half in halves:
        rows_ref[half] = mixed[:, half * 128 : (half + 1) * 128]
    for side, c in ((0, 0), (1, EDGE - 1)):
        layer = jnp.concatenate(
            [rows_ref[half, pl.ds(c, FACE, stride=EDGE)] for half in halves], axis=1
        )
        layer = layer.reshape(EDGE, EDGE, width)
        for j, entry in enumerate(three(layer, c_index(layer.shape))):
            depth_ref[side, j, pl.ds(s * FACE, FACE)] = entry

    @pl.when(last)
    def _():
        for side in range(2):
            total = jnp.zeros((listed, EDGE + 2, EDGE, width), jnp.float32)
            for i in range(3):
                product = back(
                    [depth_ref[side, j] for j in range(3)],
                    [9 * i + 3 * j + 2 * side for j in range(3)],
                ).reshape(listed, EDGE, EDGE, width)
                pieces = [product]
                if i > 0:
                    pieces.insert(0, jnp.zeros((listed, i, EDGE, width), jnp.float32))
                if i < 2:
                    pieces.append(jnp.zeros((listed, 2 - i, EDGE, width), jnp.float32))
                total = total + jnp.concatenate(pieces, axis=1)
            rows_ref[...] = jnp.zeros_like(rows_ref)
            for h in range(listed):
                n = near_ref[h, 4 + side]

                @pl.when(n < listed)
                def _():
                    piece = rounded(total[h, 1 : EDGE + 1].reshape(FACE, width))
                    c = (EDGE - 1) * (1 - side)
                    for half in halves:
                        rows_ref[half, pl.ds(c, FACE, stride=EDGE)] = piece[
                            :, half * 128 : (half + 1) * 128
                        ]
                    grad_ref[n] += jnp.concatenate([rows_ref[half] for half in halves], axis=1)

        leaving = []
        for f in range(4):
            sums = [jnp.zeros((FACE, width), jnp.float32) for _ in range(listed)]
            for h in range(listed):
                n = near_ref[h, f]
                piece = kept_ref[h, f]
                sums = [
                    total + piece * jnp.where(n == listed + t, 1.0, 0.0).astype(jnp.float32)
                    for t, total in enumerate(sums)
                ]

                @pl.when(n < listed)
                def _():
                    add_face(grad_ref, n, f, piece)

            leaving.append(sums)
        first = core_ref[0] == 0
        for t in range(listed):
            s0_ref[t] = leaving[0][t].astype(jnp.bfloat16)
            s1_ref[t] = leaving[1][t].astype(jnp.bfloat16)
            sa_ref[t] = jnp.where(first, leaving[3][t], leaving[2][t]).astype(jnp.bfloat16)
            sb_ref[t] = jnp.where(first, leaving[2][t], leaving[3][t]).astype(jnp.bfloat16)


def add_face(ref, n, f, piece):
    near_end = f % 2 == 1
    if f < 2:
        start = 0 if near_end else V - FACE
        ref[n, start : start + FACE] += piece
    else:
        for a in range(EDGE):
            start = a * FACE + (0 if near_end else FACE - EDGE)
            ref[n, start : start + EDGE] += piece[a * EDGE : (a + 1) * EDGE]


def data_call(neighbours, core, grad_in, occ_rows, weight):
    listed, _, width = grad_in.shape
    layer = jax.ShapeDtypeStruct((listed, FACE, width), jnp.bfloat16)
    return pl.pallas_call(
        data_kernel,
        grid=(listed,),
        in_specs=[smem(), smem(), by_brick((V, width)), by_brick((1, V)), whole(weight.shape)],
        out_specs=[whole((listed, V, width))] + [whole(layer.shape)] * 4,
        out_shape=[jax.ShapeDtypeStruct((listed, V, width), jnp.float32)] + [layer] * 4,
        scratch_shapes=[
            pltpu.VMEM((EDGE + 2, PLANE, width), jnp.float32),
            pltpu.VMEM((width // 128, V, 128), jnp.float32),
            pltpu.VMEM((2, 3, listed * FACE, width), jnp.bfloat16),
            pltpu.VMEM((listed, 4, FACE, width), jnp.float32),
        ],
        compiler_params=params(32),
        cost_estimate=pl.CostEstimate(
            flops=2 * listed * V * (TAPS + 3) * width * width,
            bytes_accessed=10 * MIB,
            transcendentals=0,
        ),
        name="data_gradient",
    )(neighbours, core, grad_in, occ_rows, weight)


def finish_kernel(
    core_ref, grad_ref, r0, r1, ra, rb, feat_ref, occ_ref, buf_ref, after_ref, out_ref, work_ref
):
    width = feat_ref.shape[2]
    work_ref[...] = grad_ref[...]
    first = core_ref[0] == 0
    came = (r0[0], r1[0], jnp.where(first, rb[0], ra[0]), jnp.where(first, ra[0], rb[0]))
    for f, far in enumerate(came):
        add_face(work_ref, 0, f, far.astype(jnp.float32))
    values = feat_ref[0].astype(jnp.float32)
    r = norm_scale(values)
    u = values * r
    sig = sigmoid(u)
    d_u = mask_of(occ_ref[0], width) * work_ref[0] * (sig * (1.0 + u * (1.0 - sig)))
    pulled = r * (d_u - u * jnp.mean(u * d_u, axis=-1, keepdims=True))
    out_ref[0] = (buf_ref[0].astype(jnp.float32) + pulled).astype(jnp.bfloat16)


def finish_call(core, grad, remote, features, occ_rows, grad_in, after):
    listed, _, width = features.shape
    return pl.pallas_call(
        finish_kernel,
        grid=(listed,),
        in_specs=[smem(), by_brick((V, width))]
        + [by_brick((FACE, width))] * 4
        + [by_brick((V, width)), by_brick((1, V)), by_brick((V, width))]
        + glance([after]),
        out_specs=by_brick((V, width)),
        out_shape=jax.ShapeDtypeStruct((listed, V, width), jnp.bfloat16),
        scratch_shapes=[pltpu.VMEM((1, V, width), jnp.float32)],
        compiler_params=params(16),
        cost_estimate=pl.CostEstimate(
            flops=0, bytes_accessed=10 * listed * V * width, transcendentals=listed * V * width
        ),
        name="input_gradient",
    )(core, grad, *remote, features, occ_rows, grad_in, after)


def body(features, occupancy, routes, neighbours, weight, cotangent):
    listed, _, width = features.shape
    slots = cotangent.shape[0]
    rows, columns = lax.axis_size("gx"), lax.axis_size("gy")
    depth = rows // 2
    p = lax.axis_index("gx").astype(jnp.int32)
    z, c = p // 2, p % 2
    core = c.reshape(1)
    occ_rows = occupancy.reshape(listed, 1, V)
    neighbours = inner_neighbours(neighbours, listed)
    steps = jnp.arange(slots, dtype=jnp.int32)
    def way_of(core_id):
        return 1 - 2 * core_id

    source_core = (c + steps) % 2
    from_place = (z - way_of(source_core) * (steps // 2)) % depth * 2 + source_core
    route = routes[:, 0]
    out_place = way_of(c) * (route // 2 - z) % depth * 2 + (route + c) % 2

    hidden, *layers = hidden_call(core, features, occ_rows)
    remote = [
        from_behind(layers[1], 1),
        from_behind(layers[0], -1),
        *column_pair(layers[2], layers[3]),
    ]
    came = [
        lax.all_to_all(part, "gx", 0, 0, tiled=True)
        for part in (cotangent[:, : V // 2], cotangent[:, V // 2 :])
    ]
    placed = forward_call(
        neighbours, out_place, core, hidden, layers, remote, features, occ_rows,
        weight.reshape(9, 3 * width, width), slots,
    )
    scale = float(listed * rows * columns * V) ** (-0.5)
    mine, theirs, grad_in = weight_call(
        neighbours, routes, core, hidden, layers, remote, came, occ_rows, scale, jnp.bfloat16,
        placed[0],
    )
    near, far, back = hold_call(placed[1:], came)
    near, far, back = hop(near, 1), hop(far, 1), hop(back, -1)
    near, far, back, theirs = hold_call([near, far, back, theirs], [mine])
    far = hop(far, 1)

    grad, *sends = data_call(neighbours, core, grad_in, occ_rows, weight)

    chip_sum = chip_call(mine, to_other_core(theirs), [far, grad])
    mate = to_other_core(jnp.stack([block[1] for block in (placed[0], near, far, back)]))
    same_core = [
        [(2 * layer + core_id) * columns + q for q in range(columns) for layer in range(depth)]
        for core_id in range(2)
    ]

    def all_to_all(pieces):
        return lax.all_to_all(
            pieces, ("gx", "gy"), 0, 0, axis_index_groups=same_core, tiled=True
        )

    parts = all_to_all(chip_sum.reshape(columns * depth, -1, width // 2))
    arrived = [
        from_behind(sends[0], -1), from_behind(sends[1], 1), *column_pair(sends[2], sends[3])
    ]

    token = sum(block[0, :16, :128].astype(jnp.float32) for block in [*arrived, mate])
    pieces = total_call(parts, columns * depth, [token])
    own = all_to_all(pieces)
    owned_out = collect_call(from_place, placed[0], near, far, back, mate, pieces)
    input_grad = finish_call(core, grad, arrived, features, occ_rows, grad_in, pieces)
    token = sum(block[0, :16, :128].astype(jnp.float32) for block in (owned_out, input_grad))
    own = hold_call([own], [token])[0].reshape(chip_sum.shape)
    weight_grad = half_call(core, own, False, [])
    weight_grad = half_call(core, to_other_core(own), True, [weight_grad])
    return (owned_out, input_grad, weight_grad)


def solution(mesh):
    return jax.shard_map(
        body,
        mesh=mesh,
        in_specs=(
            P(("gx", "gy"), None, None),
            P(("gx", "gy"), None),
            P(("gx", "gy"), None),
            P(("gx", "gy"), None),
            P(),
            P(("gx", "gy"), None, None),
        ),
        out_specs=(P(("gx", "gy"), None, None), P(("gx", "gy"), None, None), P()),
        check_vma=False,
    )
```

```python
import jax
import jax.numpy as jnp
from jax import lax
from jax.experimental import pallas as pl
from jax.experimental.pallas import tpu as pltpu
from jax.sharding import PartitionSpec as P

EDGE = 8
TAPS = 27
V = 512
FACE = 64
PLANE = 80
MIB = 1 << 20

norm_eps = 1e-06


def from_behind(block, distance):
    count = lax.axis_size("gx")
    return lax.ppermute(block, "gx", [(i, (i + distance) % count) for i in range(count)])


def column_pair(first, second):
    rows, columns = lax.axis_size("gx"), lax.axis_size("gy")

    def shifted(block, sign):
        ways = []
        for p in range(rows):
            step = sign if p % 2 == 0 else -sign
            ways += [(p * columns + q, p * columns + (q + step) % columns) for q in range(columns)]
        return lax.ppermute(block, ("gx", "gy"), ways)

    return shifted(first, 1), shifted(second, -1)


def inner_neighbours(neighbours, listed):
    p, q = lax.axis_index("gx"), lax.axis_index("gy")
    inside = jnp.stack(
        [p > 0, p < lax.axis_size("gx") - 1, q > 0, q < lax.axis_size("gy") - 1, True, True]
    )
    return jnp.where(inside[None, :] | (neighbours < listed), neighbours, 2 * listed)


def hop(blocks, sign):
    count = lax.axis_size("gx")
    ways = [
        (p, (p // 2 + (sign if p % 2 == 0 else -sign)) * 2 % count + p % 2)
        for p in range(count)
    ]
    return lax.ppermute(blocks, "gx", ways)


def to_other_core(block):
    return lax.ppermute(block, "gx", [(p, p ^ 1) for p in range(lax.axis_size("gx"))])


def params(limit):
    return pltpu.CompilerParams(vmem_limit_bytes=limit * MIB)


def whole(shape):
    zeros = (0,) * len(shape)
    return pl.BlockSpec(shape, lambda *_: zeros)


def by_brick(shape):
    zeros = (0,) * len(shape)
    return pl.BlockSpec((1,) + shape, lambda s, *_: (s,) + zeros)


def smem():
    return pl.BlockSpec(memory_space=pltpu.SMEM)


def anywhere():
    return pl.BlockSpec(memory_space=pl.ANY)


def glance(arrays):
    specs = []
    for array in arrays:
        zeros = (0,) * array.ndim
        block = (1,) * (array.ndim - 2) + (16, 128)
        specs.append(pl.BlockSpec(block, lambda *_, zeros=zeros: zeros))
    return specs


def mask_of(occ_row, width):
    spread = jnp.broadcast_to(occ_row.astype(jnp.float32), (128, V))
    column = jnp.transpose(spread)
    return jnp.concatenate([column] * (width // 128), axis=1)


def norm_scale(values):
    return lax.rsqrt(jnp.mean(values * values, axis=-1, keepdims=True) + norm_eps)


def sigmoid(u):
    return 1.0 / (1.0 + jnp.exp(-u))


def hidden_kernel(core_ref, feat_ref, occ_ref, hid_ref, x0_ref, x1_ref, ya_ref, yb_ref):
    width = feat_ref.shape[2]
    values = feat_ref[0].astype(jnp.float32)
    u = values * norm_scale(values)
    hidden = mask_of(occ_ref[0], width) * (u * sigmoid(u))
    hid_ref[0] = hidden.astype(jnp.bfloat16)
    cube = hidden.reshape(EDGE, EDGE, EDGE, width)
    x0_ref[0] = cube[0].reshape(FACE, width).astype(jnp.bfloat16)
    x1_ref[0] = cube[EDGE - 1].reshape(FACE, width).astype(jnp.bfloat16)
    first = core_ref[0] == 0
    low, high = cube[:, 0].reshape(FACE, width), cube[:, EDGE - 1].reshape(FACE, width)
    ya_ref[0] = jnp.where(first, high, low).astype(jnp.bfloat16)
    yb_ref[0] = jnp.where(first, low, high).astype(jnp.bfloat16)


def hidden_call(core, features, occ_rows):
    listed, _, width = features.shape
    layer = jax.ShapeDtypeStruct((listed, FACE, width), jnp.bfloat16)
    return pl.pallas_call(
        hidden_kernel,
        grid=(listed,),
        in_specs=[smem(), by_brick((V, width)), by_brick((1, V))],
        out_specs=[by_brick((V, width))] + [by_brick((FACE, width))] * 4,
        out_shape=[jax.ShapeDtypeStruct((listed, V, width), jnp.bfloat16)] + [layer] * 4,
        compiler_params=params(16),
        name="hidden",
    )(core, features, occ_rows)


def hold_kernel(*refs):
    pass


def hold_call(blocks, after):
    return pl.pallas_call(
        hold_kernel,
        grid=(1,),
        in_specs=[anywhere()] * len(blocks) + glance(after),
        out_specs=[anywhere()] * len(blocks),
        out_shape=[jax.ShapeDtypeStruct(block.shape, block.dtype) for block in blocks],
        input_output_aliases={i: i for i in range(len(blocks))},
        compiler_params=params(16),
        name="hold",
    )(*blocks, *after)


def collect_kernel(
    place_ref, own_ref, near_ref, far_ref, back_ref, mate_ref, after_ref, out_ref
):
    for step, came_ref in enumerate((own_ref, near_ref, far_ref, back_ref)):
        out_ref[place_ref[2 * step]] = came_ref[0]
        out_ref[place_ref[2 * step + 1]] = mate_ref[step]


def collect_call(place, own, near, far, back, mate, after):
    shape = (2 * mate.shape[0],) + mate.shape[1:]
    return pl.pallas_call(
        collect_kernel,
        grid=(1,),
        in_specs=[smem()] + [whole(own.shape)] * 4 + [whole(mate.shape)] + glance([after]),
        out_specs=whole(shape),
        out_shape=jax.ShapeDtypeStruct(shape, mate.dtype),
        compiler_params=params(56),
        cost_estimate=pl.CostEstimate(
            flops=0, bytes_accessed=4 * shape[0] * shape[1] * shape[2], transcendentals=0
        ),
        name="collect",
    )(place, own, near, far, back, mate, after)


def roll_c(block, shift):
    flat = block.reshape((-1,) + block.shape[-2:])
    return pltpu.roll(flat, shift % EDGE, 1).reshape(block.shape)


def c_index(shape):
    return lax.broadcasted_iota(jnp.int32, shape, len(shape) - 2)


def extended_brick(s, near_ref, core_ref, hid_ref, own, far, store):
    listed, _, width = hid_ref.shape

    def flag(condition):
        return jnp.where(condition, 1.0, 0.0).astype(jnp.float32)

    first = core_ref[0] == 0

    def face(f):
        n = near_ref[s, f]
        at_here, at_there = jnp.minimum(n, listed - 1), jnp.clip(n - listed, 0, listed - 1)
        if f < 2:
            here, there = own[f ^ 1][at_here], far[f][at_there]
        else:
            a, b = (2, 3) if f == 2 else (3, 2)
            here = jnp.where(first, own[a][at_here], own[b][at_here])
            there = jnp.where(first, far[a][at_there], far[b][at_there])
        here, there = here.astype(jnp.float32), there.astype(jnp.float32)
        value = here * flag(n < listed) + there * flag((n >= listed) & (n < 2 * listed))
        return value.reshape(EDGE, EDGE, width)

    def column(f):
        n = near_ref[s, f]
        brick = hid_ref[jnp.minimum(n, listed - 1)].astype(jnp.float32) * flag(n < listed)
        return brick.reshape(EDGE, EDGE, EDGE, width)

    def extended(core, sides):
        x0, x1, y0, y1 = sides
        blank = jnp.zeros((1, EDGE, width), jnp.float32)
        middle = jnp.concatenate([y0[:, None], core, y1[:, None]], axis=1)
        first = jnp.concatenate([blank, x0, blank], axis=0)[None]
        last = jnp.concatenate([blank, x1, blank], axis=0)[None]
        return jnp.concatenate([first, middle, last], axis=0)

    def put(k, block):
        everything = block.reshape(EDGE + 2, PLANE, width).astype(jnp.bfloat16)
        inner = block[:, 1 : EDGE + 1].reshape(EDGE + 2, FACE, width).astype(jnp.bfloat16)
        store(k, everything, inner)

    core = hid_ref[s].astype(jnp.float32).reshape(EDGE, EDGE, EDGE, width)
    sides = [face(f) for f in range(4)]
    at = c_index(core.shape)
    at_side = c_index(sides[0].shape)
    for k, edge, f in ((0, EDGE - 1, 4), (2, 0, 5)):
        shown = extended(
            jnp.where(at == edge, column(f), core),
            [jnp.where(at_side == edge, 0.0, side) for side in sides],
        )
        put(k, roll_c(shown, 1 - k))
    put(1, extended(core, sides))


def window(even_ref, odd_ref, s, i, j, k):
    if j == 1:
        part = odd_ref[s, k, pl.ds(i, EDGE)]
    else:
        part = even_ref[s, k, pl.ds(i, EDGE), j * EDGE : j * EDGE + FACE]
    return part.reshape(V, part.shape[-1])


def forward_kernel(
    near_ref, place_ref, core_ref, hid_ref, l0, l1, l2, l3, r0, r1, r2, r3, feat_ref, occ_ref, w_ref,
    *refs,
):
    outs, even_ref, odd_ref = refs[:-2], refs[-2], refs[-1]
    s = pl.program_id(0)
    width = feat_ref.shape[2]

    @pl.when(s == 0)
    def _():
        for out_ref in outs:
            out_ref[...] = jnp.zeros_like(out_ref)

    def store(k, everything, inner):
        even_ref[0, k] = everything
        odd_ref[0, k] = inner

    extended_brick(s, near_ref, core_ref, hid_ref, (l0, l1, l2, l3), (r0, r1, r2, r3), store)
    total = jnp.zeros((V, width), jnp.float32)
    for i in range(3):
        for j in range(3):
            rows = jnp.concatenate(
                [window(even_ref, odd_ref, 0, i, j, k) for k in range(3)], axis=1
            )
            total = total + jnp.dot(rows, w_ref[3 * i + j], preferred_element_type=jnp.float32)
    result = feat_ref[0].astype(jnp.float32) + mask_of(occ_ref[0], width) * total
    result = result.astype(jnp.bfloat16)
    for step, out_ref in enumerate(outs):

        @pl.when(place_ref[s] // 2 == step)
        def _():
            out_ref[place_ref[s] % 2] = result


def extended_scratch(bricks, width):
    return [
        pltpu.VMEM((bricks, 3, EDGE + 2, PLANE, width), jnp.bfloat16),
        pltpu.VMEM((bricks, 3, EDGE + 2, FACE, width), jnp.bfloat16),
    ]


def forward_call(
    neighbours, place, core, hidden, layers, remote, features, occ_rows, weight9, slots
):
    listed, _, width = features.shape
    layer = whole((listed, FACE, width))
    return pl.pallas_call(
        forward_kernel,
        grid=(listed,),
        in_specs=[smem(), smem(), smem(), whole((listed, V, width))]
        + [layer] * 8
        + [by_brick((V, width)), by_brick((1, V)), whole(weight9.shape)],
        out_specs=[whole((2, V, width))] * (slots // 2),
        out_shape=[jax.ShapeDtypeStruct((2, V, width), jnp.bfloat16)] * (slots // 2),
        scratch_shapes=extended_scratch(1, width),
        compiler_params=params(56),
        cost_estimate=pl.CostEstimate(
            flops=2 * listed * V * TAPS * width * width,
            bytes_accessed=10 * MIB,
            transcendentals=0,
        ),
        name="forward",
    )(neighbours, place, core, hidden, *layers, *remote, features, occ_rows, weight9)


def weight_kernel(
    near_ref, place_ref, core_ref, hid_ref, l0, l1, l2, l3, r0, r1, r2, r3, occ_ref, after_ref,
    *refs, scale,
):
    came, refs = refs[:-7], refs[-7:]
    mine_ref, theirs_ref, grad_ref, even_ref, odd_ref, turned_ref, sem = refs
    part = V // len(came)
    i = pl.program_id(0)
    listed, _, width = hid_ref.shape
    half = width // 2

    def copy(t, s):
        return pltpu.make_async_copy(
            came[t].at[place_ref[s, 0]],
            grad_ref.at[s, pl.ds(t * part, part)],
            sem.at[t * listed + s],
        )

    @pl.when(i == 0)
    def _():
        for s in range(listed):
            for t in range(len(came)):
                copy(t, s).start()

        @pl.loop(0, listed)
        def _(s):
            def store(k, everything, inner):
                even_ref[s, k] = everything
                odd_ref[s, k] = inner

            extended_brick(s, near_ref, core_ref, hid_ref, (l0, l1, l2, l3), (r0, r1, r2, r3), store)

        for s in range(listed):
            for t in range(len(came)):
                copy(t, s).wait()
            mixed = grad_ref[s].astype(jnp.float32) * mask_of(occ_ref[s], width)
            turned_ref[:, s * V : (s + 1) * V] = jnp.transpose(mixed).astype(jnp.bfloat16)

    @pl.when(i < 3)
    def _():
        first = core_ref[0] == 0
        for j in range(3):
            for k in range(3):
                rows = jnp.concatenate(
                    [window(even_ref, odd_ref, s, i, j, k) for s in range(listed)], axis=0
                )
                product = jnp.dot(turned_ref[...], rows, preferred_element_type=jnp.float32)
                product = jnp.transpose(product) * scale
                low, high = product[:, :half], product[:, half:]
                mine_ref[3 * j + k] = jnp.where(first, low, high)
                theirs_ref[3 * j + k] = jnp.where(first, high, low).astype(theirs_ref.dtype)

    @pl.when(i == 3)
    def _():
        mine_ref[...] = jnp.zeros_like(mine_ref)
        theirs_ref[...] = jnp.zeros_like(theirs_ref)


def weight_call(
    neighbours, place, core, hidden, layers, remote, came, occ_rows, scale, kind, after
):
    listed, _, width = hidden.shape
    shape = (TAPS + 1, width, width // 2)
    block = pl.BlockSpec((9, width, width // 2), lambda i: (i, 0, 0))
    return pl.pallas_call(
        lambda *refs: weight_kernel(*refs, scale=scale),
        grid=(4,),
        in_specs=[smem(), smem(), smem(), whole(hidden.shape)]
        + [whole((listed, FACE, width))] * 8
        + [whole(occ_rows.shape)]
        + glance([after])
        + [anywhere()] * len(came),
        out_specs=[block, block, whole(hidden.shape)],
        out_shape=[
            jax.ShapeDtypeStruct(shape, jnp.float32),
            jax.ShapeDtypeStruct(shape, kind),
            jax.ShapeDtypeStruct(hidden.shape, jnp.bfloat16),
        ],
        scratch_shapes=extended_scratch(listed, width)
        + [pltpu.VMEM((width, listed * V), jnp.bfloat16), pltpu.SemaphoreType.DMA((len(came) * listed,))],
        compiler_params=params(32),
        cost_estimate=pl.CostEstimate(
            flops=2 * listed * V * TAPS * width * width,
            bytes_accessed=10 * MIB,
            transcendentals=0,
        ),
        name="weight_gradient",
    )(neighbours, place, core, hidden, *layers, *remote, occ_rows, after, *came)


def chip_kernel(mine_ref, theirs_ref, *refs):
    out_ref = refs[-1]
    added = mine_ref[...] + theirs_ref[...].astype(jnp.float32)
    out_ref[...] = added.astype(jnp.bfloat16)


def chip_call(mine, theirs, after):
    taps, width, half = mine.shape
    block = pl.BlockSpec((7, width, half), lambda t: (t, 0, 0))
    return pl.pallas_call(
        chip_kernel,
        grid=(taps // 7,),
        in_specs=[block, block] + glance(after),
        out_specs=block,
        out_shape=jax.ShapeDtypeStruct(mine.shape, jnp.bfloat16),
        compiler_params=params(12),
        name="chip_sum",
    )(mine, theirs, *after)


def total_kernel(parts_ref, *refs):
    out_ref = refs[-1]
    total = jnp.sum(parts_ref[...].astype(jnp.float32), axis=0)
    for z in range(out_ref.shape[0]):
        out_ref[z] = total.astype(jnp.bfloat16)


def total_call(parts, copies, after):
    _, rows, half = parts.shape
    return pl.pallas_call(
        total_kernel,
        grid=(1,),
        in_specs=[whole(parts.shape)] + glance(after),
        out_specs=whole((copies, rows, half)),
        out_shape=jax.ShapeDtypeStruct((copies, rows, half), jnp.bfloat16),
        compiler_params=params(20),
        name="total",
    )(parts, *after)


def half_kernel(core_ref, block_ref, *refs):
    refs[-1][...] = block_ref[...].astype(jnp.float32)


def half_call(core, block, is_other, base):
    _, width, half = block.shape

    def place(t, core_ref):
        return t, 0, (1 - core_ref[0] if is_other else core_ref[0])

    return pl.pallas_call(
        half_kernel,
        grid_spec=pltpu.PrefetchScalarGridSpec(
            num_scalar_prefetch=1,
            grid=(TAPS // 9,),
            in_specs=[pl.BlockSpec((9, width, half), lambda t, core_ref: (t, 0, 0))]
            + [anywhere()] * len(base),
            out_specs=pl.BlockSpec((9, width, half), place),
        ),
        out_shape=jax.ShapeDtypeStruct((TAPS, width, 2 * half), jnp.float32),
        input_output_aliases={2: 0} if base else {},
        compiler_params=params(16),
        cost_estimate=pl.CostEstimate(
            flops=0, bytes_accessed=6 * TAPS * width * half, transcendentals=0
        ),
        name="half",
    )(core, block, *base)


def data_kernel(
    near_ref, core_ref, buf_ref, occ_ref, w_ref,
    grad_ref, s0_ref, s1_ref, sa_ref, sb_ref,
    wide_ref, rows_ref, depth_ref, kept_ref,
):
    s = pl.program_id(0)
    listed = grad_ref.shape[0]
    width = buf_ref.shape[2]
    last = s == listed - 1

    mixed = buf_ref[0].astype(jnp.float32) * mask_of(occ_ref[0], width)
    cube = mixed.reshape(FACE, EDGE, width)
    at = c_index(cube.shape)

    def three(block, index):
        ahead = jnp.where(index == EDGE - 1, 0.0, roll_c(block, -1))
        behind = jnp.where(index == 0, 0.0, roll_c(block, 1))
        flat = (-1, width)
        return [entry.reshape(flat).astype(jnp.bfloat16) for entry in (ahead, block, behind)]

    def back(rows, taps):
        return sum(
            lax.dot_general(
                row, w_ref[tap], (((1,), (1,)), ((), ())), preferred_element_type=jnp.float32
            )
            for row, tap in zip(rows, taps)
        )

    rows = three(cube, at)
    wide_ref[...] = jnp.zeros_like(wide_ref)
    for i in range(3):
        for j in range(3):
            product = back(rows, [9 * i + 3 * j + k for k in range(3)])
            wide_ref[i : i + EDGE, j * EDGE : j * EDGE + FACE] += product.reshape(
                EDGE, FACE, width
            )

    def rounded(block):
        return block.astype(jnp.bfloat16).astype(jnp.float32)

    inside = slice(EDGE, EDGE + FACE)
    grad_ref[s] = rounded(wide_ref[1 : EDGE + 1, inside].reshape(V, width))
    kept_ref[s, 0] = rounded(wide_ref[0, inside])
    kept_ref[s, 1] = rounded(wide_ref[EDGE + 1, inside])
    kept_ref[s, 2] = rounded(wide_ref[1 : EDGE + 1, 0:EDGE].reshape(FACE, width))
    kept_ref[s, 3] = rounded(wide_ref[1 : EDGE + 1, PLANE - EDGE : PLANE].reshape(FACE, width))

    halves = range(width // 128)
    for half in halves:
        rows_ref[half] = mixed[:, half * 128 : (half + 1) * 128]
    for side, c in ((0, 0), (1, EDGE - 1)):
        layer = jnp.concatenate(
            [rows_ref[half, pl.ds(c, FACE, stride=EDGE)] for half in halves], axis=1
        )
        layer = layer.reshape(EDGE, EDGE, width)
        for j, entry in enumerate(three(layer, c_index(layer.shape))):
            depth_ref[side, j, pl.ds(s * FACE, FACE)] = entry

    @pl.when(last)
    def _():
        for side in range(2):
            total = jnp.zeros((listed, EDGE + 2, EDGE, width), jnp.float32)
            for i in range(3):
                product = back(
                    [depth_ref[side, j] for j in range(3)],
                    [9 * i + 3 * j + 2 * side for j in range(3)],
                ).reshape(listed, EDGE, EDGE, width)
                pieces = [product]
                if i > 0:
                    pieces.insert(0, jnp.zeros((listed, i, EDGE, width), jnp.float32))
                if i < 2:
                    pieces.append(jnp.zeros((listed, 2 - i, EDGE, width), jnp.float32))
                total = total + jnp.concatenate(pieces, axis=1)
            rows_ref[...] = jnp.zeros_like(rows_ref)
            for h in range(listed):
                n = near_ref[h, 4 + side]

                @pl.when(n < listed)
                def _():
                    piece = rounded(total[h, 1 : EDGE + 1].reshape(FACE, width))
                    c = (EDGE - 1) * (1 - side)
                    for half in halves:
                        rows_ref[half, pl.ds(c, FACE, stride=EDGE)] = piece[
                            :, half * 128 : (half + 1) * 128
                        ]
                    grad_ref[n] += jnp.concatenate([rows_ref[half] for half in halves], axis=1)

        leaving = []
        for f in range(4):
            sums = [jnp.zeros((FACE, width), jnp.float32) for _ in range(listed)]
            for h in range(listed):
                n = near_ref[h, f]
                piece = kept_ref[h, f]
                sums = [
                    total + piece * jnp.where(n == listed + t, 1.0, 0.0).astype(jnp.float32)
                    for t, total in enumerate(sums)
                ]

                @pl.when(n < listed)
                def _():
                    add_face(grad_ref, n, f, piece)

            leaving.append(sums)
        first = core_ref[0] == 0
        for t in range(listed):
            s0_ref[t] = leaving[0][t].astype(jnp.bfloat16)
            s1_ref[t] = leaving[1][t].astype(jnp.bfloat16)
            sa_ref[t] = jnp.where(first, leaving[3][t], leaving[2][t]).astype(jnp.bfloat16)
            sb_ref[t] = jnp.where(first, leaving[2][t], leaving[3][t]).astype(jnp.bfloat16)


def add_face(ref, n, f, piece):
    near_end = f % 2 == 1
    if f < 2:
        start = 0 if near_end else V - FACE
        ref[n, start : start + FACE] += piece
    else:
        for a in range(EDGE):
            start = a * FACE + (0 if near_end else FACE - EDGE)
            ref[n, start : start + EDGE] += piece[a * EDGE : (a + 1) * EDGE]


def data_call(neighbours, core, grad_in, occ_rows, weight):
    listed, _, width = grad_in.shape
    layer = jax.ShapeDtypeStruct((listed, FACE, width), jnp.bfloat16)
    return pl.pallas_call(
        data_kernel,
        grid=(listed,),
        in_specs=[smem(), smem(), by_brick((V, width)), by_brick((1, V)), whole(weight.shape)],
        out_specs=[whole((listed, V, width))] + [whole(layer.shape)] * 4,
        out_shape=[jax.ShapeDtypeStruct((listed, V, width), jnp.float32)] + [layer] * 4,
        scratch_shapes=[
            pltpu.VMEM((EDGE + 2, PLANE, width), jnp.float32),
            pltpu.VMEM((width // 128, V, 128), jnp.float32),
            pltpu.VMEM((2, 3, listed * FACE, width), jnp.bfloat16),
            pltpu.VMEM((listed, 4, FACE, width), jnp.float32),
        ],
        compiler_params=params(32),
        cost_estimate=pl.CostEstimate(
            flops=2 * listed * V * (TAPS + 3) * width * width,
            bytes_accessed=10 * MIB,
            transcendentals=0,
        ),
        name="data_gradient",
    )(neighbours, core, grad_in, occ_rows, weight)


def finish_kernel(
    core_ref, grad_ref, r0, r1, ra, rb, feat_ref, occ_ref, buf_ref, after_ref, out_ref, work_ref
):
    width = feat_ref.shape[2]
    work_ref[...] = grad_ref[...]
    first = core_ref[0] == 0
    came = (r0[0], r1[0], jnp.where(first, rb[0], ra[0]), jnp.where(first, ra[0], rb[0]))
    for f, far in enumerate(came):
        add_face(work_ref, 0, f, far.astype(jnp.float32))
    values = feat_ref[0].astype(jnp.float32)
    r = norm_scale(values)
    u = values * r
    sig = sigmoid(u)
    d_u = mask_of(occ_ref[0], width) * work_ref[0] * (sig * (1.0 + u * (1.0 - sig)))
    pulled = r * (d_u - u * jnp.mean(u * d_u, axis=-1, keepdims=True))
    out_ref[0] = (buf_ref[0].astype(jnp.float32) + pulled).astype(jnp.bfloat16)


def finish_call(core, grad, remote, features, occ_rows, grad_in, after):
    listed, _, width = features.shape
    return pl.pallas_call(
        finish_kernel,
        grid=(listed,),
        in_specs=[smem(), by_brick((V, width))]
        + [by_brick((FACE, width))] * 4
        + [by_brick((V, width)), by_brick((1, V)), by_brick((V, width))]
        + glance([after]),
        out_specs=by_brick((V, width)),
        out_shape=jax.ShapeDtypeStruct((listed, V, width), jnp.bfloat16),
        scratch_shapes=[pltpu.VMEM((1, V, width), jnp.float32)],
        compiler_params=params(56),
        cost_estimate=pl.CostEstimate(
            flops=0, bytes_accessed=10 * listed * V * width, transcendentals=listed * V * width
        ),
        name="input_gradient",
    )(core, grad, *remote, features, occ_rows, grad_in, after)


def body(features, occupancy, routes, neighbours, weight, cotangent):
    listed, _, width = features.shape
    slots = cotangent.shape[0]
    rows, columns = lax.axis_size("gx"), lax.axis_size("gy")
    depth = rows // 2
    p = lax.axis_index("gx").astype(jnp.int32)
    z, c = p // 2, p % 2
    core = c.reshape(1)
    occ_rows = occupancy.reshape(listed, 1, V)
    neighbours = inner_neighbours(neighbours, listed)
    steps = jnp.arange(slots, dtype=jnp.int32)
    def way_of(core_id):
        return 1 - 2 * core_id

    source_core = (c + steps) % 2
    from_place = (z - way_of(source_core) * (steps // 2)) % depth * 2 + source_core
    route = routes[:, 0]
    out_place = way_of(c) * (route // 2 - z) % depth * 2 + (route + c) % 2

    hidden, *layers = hidden_call(core, features, occ_rows)
    remote = [
        from_behind(layers[1], 1),
        from_behind(layers[0], -1),
        *column_pair(layers[2], layers[3]),
    ]
    came = [
        lax.all_to_all(part, "gx", 0, 0, tiled=True)
        for part in (cotangent[:, : V // 2], cotangent[:, V // 2 :])
    ]
    placed = forward_call(
        neighbours, out_place, core, hidden, layers, remote, features, occ_rows,
        weight.reshape(9, 3 * width, width), slots,
    )
    scale = float(listed * rows * columns * V) ** (-0.5)
    mine, theirs, grad_in = weight_call(
        neighbours, routes, core, hidden, layers, remote, came, occ_rows, scale, jnp.bfloat16,
        placed[0],
    )
    near, far, back = hold_call(placed[1:], came)
    near, far, back = hop(near, 1), hop(far, 1), hop(back, -1)
    near, far, back, theirs = hold_call([near, far, back, theirs], [mine])
    far = hop(far, 1)

    grad, *sends = data_call(neighbours, core, grad_in, occ_rows, weight)

    chip_sum = chip_call(mine, to_other_core(theirs), [far, grad])
    mate = to_other_core(jnp.stack([block[1] for block in (placed[0], near, far, back)]))
    same_core = [
        [(2 * layer + core_id) * columns + q for q in range(columns) for layer in range(depth)]
        for core_id in range(2)
    ]

    def all_to_all(pieces):
        return lax.all_to_all(
            pieces, ("gx", "gy"), 0, 0, axis_index_groups=same_core, tiled=True
        )

    parts = all_to_all(chip_sum.reshape(columns * depth, -1, width // 2))
    arrived = [
        from_behind(sends[0], -1), from_behind(sends[1], 1), *column_pair(sends[2], sends[3])
    ]

    token = sum(block[0, :16, :128].astype(jnp.float32) for block in [*arrived, mate])
    pieces = total_call(parts, columns * depth, [token])
    own = all_to_all(pieces)
    owned_out = collect_call(from_place, placed[0], near, far, back, mate, pieces)
    input_grad = finish_call(core, grad, arrived, features, occ_rows, grad_in, pieces)
    token = sum(block[0, :16, :128].astype(jnp.float32) for block in (owned_out, input_grad))
    own = hold_call([own], [token])[0].reshape(chip_sum.shape)
    weight_grad = half_call(core, own, False, [])
    weight_grad = half_call(core, to_other_core(own), True, [weight_grad])
    return (owned_out, input_grad, weight_grad)


def solution(mesh):
    return jax.shard_map(
        body,
        mesh=mesh,
        in_specs=(
            P(("gx", "gy"), None, None),
            P(("gx", "gy"), None),
            P(("gx", "gy"), None),
            P(("gx", "gy"), None),
            P(),
            P(("gx", "gy"), None, None),
        ),
        out_specs=(P(("gx", "gy"), None, None), P(("gx", "gy"), None, None), P()),
        check_vma=False,
    )
```
